512 devices in a mesh: tm: 16 (over x, z_lo), height: 4 (over y), head: 8 (over z_hi, core).
Axes of the slice: x: 4, y: 4, z: 16 (z_hi: 4, z_lo: 4; z = z_hi * 4 + z_lo), core: 2. Of those that a mesh axis runs over, the one named last changes fastest.
Arguments:
- queries: bfloat16 [16, 4, 384, 3072], P('tm', 'height', 'head'), may hold values from -6 to 6
- keys: bfloat16 [16, 4, 384, 3072], P('tm', 'height', 'head'), may hold values from -6 to 6
- values: bfloat16 [16, 4, 384, 3072], P('tm', 'height', 'head'), may hold values from -18 to 18
- q_gain: float32 [128], replicated, may hold values from 1 to 2
- k_gain: float32 [128], replicated, may hold values from 1 to 2
- offsets: int32 [16, 4, 1, 8], P('tm', 'height'), may hold values from 0 to 26, as said below
- counts: int32 [16, 4, 1], P('tm', 'height'), may hold values from 1 to 8, as said below
Outputs:
- attended: bfloat16 [16, 4, 384, 3072], P('tm', 'height', 'head')
The draws below stay inside these ranges and needn't reach their ends.
Inputs may be any that keep to these rules, and one draw needn't show every extreme that they name: `offsets`: the 8 entries of a tile are distinct codes e; entry 0 is 13, the tile itself, and every live entry names a tile inside the grid of 4 x 4 x 4 tiles. `counts`: A tile's count is at least one more than the number of its face neighbours inside the grid and at most the number of its neighbouring tiles (itself included) inside the grid.
All inputs are finite; a program needn't handle non-finite values.
Results may differ from the reference program's by a relative error of at most 0.01.
Values may be sent and summed in bfloat16 or wider, within the bound.
No kernel may reach another device: no remote copies, remote signals or barrier semaphores. Data moves between devices by JAX's collectives and lax.ppermute only.
A program may use at most 128 MiB of HBM per device.

```python
import math
from functools import partial
import jax
import jax.numpy as jnp
from jax import lax

HEADS = 24
HD = 128
D = 3072
TILE = 384
TILES_T = 4
WT = 1
SLOTS = 8
CB = 4
BLOCKS = 16
COLS = 4
TILES_H = 4
GROUP_TOK = 384


def tile_layout():
    all_codes = jnp.arange(27, dtype=jnp.int32)
    step_t = all_codes // 9 - 1
    step_h = all_codes // 3 % 3 - 1
    step_w = all_codes % 3 - 1
    block_pos = jnp.arange(BLOCKS, dtype=jnp.int32)
    frame_pos = (block_pos // CB)[:, None, None, None]
    row_pos = jnp.arange(TILES_H, dtype=jnp.int32)[None, :, None, None]
    column_pos = (block_pos % CB)[:, None, None, None] * WT + jnp.arange(WT, dtype=jnp.int32)[None, None, :, None]
    inside = (frame_pos + step_t >= 0) & (frame_pos + step_t < TILES_T)
    inside = inside & (row_pos + step_h >= 0) & (row_pos + step_h < TILES_H)
    inside = inside & (column_pos + step_w >= 0) & (column_pos + step_w < COLS)
    facing = jnp.abs(step_t) + jnp.abs(step_h) + jnp.abs(step_w) == 1
    facing = jnp.broadcast_to(facing, inside.shape) & inside
    return (all_codes, inside, facing)


def draw_offsets(key, part):
    key = jax.random.fold_in(key, 5)
    all_codes, inside, facing = tile_layout()
    raw_bits = jax.random.randint(key, (BLOCKS, TILES_H, WT, 27), 0, 1 << 20)
    ranking = raw_bits * 32 + all_codes
    ranking = jnp.where(facing, ranking - (1 << 25), ranking)
    ranking = jnp.where(inside, ranking, ranking + (1 << 26))
    ranking = jnp.where(all_codes == 13, -(1 << 27), ranking)
    order_of = jnp.argsort(ranking, axis=-1, stable=True)
    return order_of[..., :SLOTS].astype(jnp.int32)


def draw_counts(key, part):
    key = jax.random.fold_in(key, 7)
    key_cap, key_raw, key_pick = jax.random.split(key, 3)
    all_codes, inside, facing = tile_layout()
    inside_count = jnp.sum(inside.astype(jnp.int32), axis=-1)
    least = jnp.minimum(1 + jnp.sum(facing.astype(jnp.int32), axis=-1), SLOTS)
    most = jnp.minimum(inside_count, SLOTS)
    span = jnp.maximum(most - least, 0)
    device_cap = jax.random.randint(key_cap, (BLOCKS, TILES_H, 1), 0, SLOTS)
    raw_bits = jax.random.randint(key_raw, (BLOCKS, TILES_H, WT), 0, 1 << 20)
    drawn = (least + raw_bits % (jnp.minimum(span, device_cap) + 1)).reshape(-1)
    flat_pos = jnp.arange(drawn.shape[0], dtype=jnp.int32)
    pick_bits = jax.random.randint(key_pick, drawn.shape, 0, 1 << 20)
    eligible = inside_count.reshape(-1) >= SLOTS
    scores = jnp.where(eligible, pick_bits * 1024 + flat_pos % 1024, -1)
    picked = jnp.argmax(scores)
    drawn = jnp.where(flat_pos == picked, SLOTS, drawn)
    return drawn.reshape(BLOCKS, TILES_H, WT).astype(jnp.int32)


def level_of(own_key, shape, pieces, low, top_value):
    def one(dim, blocks):
        draws = jax.random.uniform(jax.random.fold_in(jax.random.fold_in(own_key, 6), dim), (blocks,), jnp.float32, low / len(pieces), top_value / len(pieces))
        return jnp.repeat(jnp.exp(draws), shape[dim] // blocks).reshape((-1,) + (1,) * (len(shape) - dim - 1))

    level = one(*pieces[0])
    for cut in pieces[1:]:
        level = level * one(*cut)
    return level


def bell_draw(rng, shape, deviation, most, cuts=(), held_as=jnp.bfloat16):
    result = deviation * jax.random.normal(rng, shape, jnp.float32)
    if cuts:
        result = result * level_of(rng, shape, cuts, -0.22, 0.18)
    return jnp.clip(result, -most, most).astype(held_as)


def setup_inputs(seed: int = 0) -> dict:
    key_of = jax.random.split(jax.random.key(seed), 8)
    queries = bell_draw(key_of[0], (BLOCKS, TILES_H, GROUP_TOK, D), 1.0, 6.0, ((0, 16), (1, 4), (2, 8)))
    keys = bell_draw(key_of[1], (BLOCKS, TILES_H, GROUP_TOK, D), 1.0, 6.0, ((0, 16), (1, 4), (2, 8)))
    values = bell_draw(key_of[2], (BLOCKS, TILES_H, GROUP_TOK, D), 3.0, 18.0, ((0, 16), (1, 4), (2, 8)))
    q_gain = jnp.clip(jnp.exp(jax.random.uniform(key_of[3], (HD,), jnp.float32, math.log(1.0), math.log(2.0))), 1.0, 2.0)
    k_gain = jnp.clip(jnp.exp(jax.random.uniform(key_of[4], (HD,), jnp.float32, math.log(1.0), math.log(2.0))), 1.0, 2.0)
    offsets = draw_offsets(jax.random.fold_in(key_of[7], 71), 0)
    counts = draw_counts(jax.random.fold_in(key_of[7], 71), 0)
    return dict(queries=queries, keys=keys, values=values, q_gain=q_gain, k_gain=k_gain, offsets=offsets, counts=counts)


def normalize(tokens, gain):
    dims_in = tokens.shape
    head_width = gain.shape[0]
    by_head = tokens.astype(jnp.float32).reshape(dims_in[:-1] + (dims_in[-1] // head_width, head_width))
    mean_sq = lax.optimization_barrier(jnp.mean(by_head * by_head, axis=-1, keepdims=True))
    scaled = by_head * lax.rsqrt(mean_sq + 1e-06) * gain.astype(jnp.float32)
    return scaled.astype(jnp.bfloat16).reshape(dims_in)

def to_grid(tokens):
    width = tokens.shape[-1]
    split = tokens.reshape(TILES_T, CB, TILES_H, WT, TILE, width)
    return split.transpose(0, 2, 1, 3, 4, 5).reshape(TILES_T, TILES_H, COLS, TILE, width)

def fetch_tile(source, frame_at, row_at, column_at):
    zero_at = jnp.int32(0)
    tile_block = lax.dynamic_slice(source, (frame_at, row_at, column_at, zero_at, zero_at), (1, 1, 1, TILE, D))
    return tile_block.reshape(TILE, HEADS, HD).astype(jnp.float32)

def reference(queries, keys, values, q_gain, k_gain, offsets, counts):
    norm_q = to_grid(normalize(queries, q_gain)).reshape(TILES_T, TILES_H, COLS, TILE, HEADS, HD)
    norm_k = to_grid(normalize(keys, k_gain))
    plain_v = to_grid(values)
    grid_offsets = offsets.reshape(TILES_T, CB, TILES_H, WT, SLOTS).transpose(0, 2, 1, 3, 4).reshape(TILES_T, TILES_H, COLS, SLOTS)
    grid_counts = counts.reshape(TILES_T, CB, TILES_H, WT).transpose(0, 2, 1, 3).reshape(TILES_T, TILES_H, COLS)
    score_scale = 1.0 / math.sqrt(HD)
    column_base = jnp.arange(COLS, dtype=jnp.int32)

    def one_block(block_index):
        frame_tile = block_index // TILES_H
        row_tile = block_index % TILES_H
        query_tiles = norm_q[frame_tile, row_tile].astype(jnp.float32)
        slot_codes = grid_offsets[frame_tile, row_tile]
        live_counts = grid_counts[frame_tile, row_tile]

        def slot_step(slot_index, totals):
            numerator, denominator = totals
            slot_code = slot_codes[:, slot_index]
            frame_at = frame_tile + slot_code // 9 - 1
            row_at = row_tile + slot_code // 3 % 3 - 1
            column_at = column_base + slot_code % 3 - 1
            key_tiles = jax.vmap(partial(fetch_tile, norm_k))(frame_at, row_at, column_at)
            value_tiles = jax.vmap(partial(fetch_tile, plain_v))(frame_at, row_at, column_at)
            scores = jnp.einsum('wqhd,wkhd->wqhk', query_tiles, key_tiles) * score_scale
            live_mask = (slot_index < live_counts).astype(jnp.float32)
            weights = jnp.exp(scores) * live_mask[:, None, None, None]
            rounded = lax.optimization_barrier(weights.astype(jnp.bfloat16)).astype(jnp.float32)
            numerator = numerator + jnp.einsum('wqhk,wkhd->wqhd', rounded, value_tiles)
            denominator = denominator + lax.optimization_barrier(jnp.sum(weights, axis=-1))
            return (numerator, denominator)
        initial = (jnp.zeros((COLS, TILE, HEADS, HD), jnp.float32), jnp.zeros((COLS, TILE, HEADS), jnp.float32))
        numerator, denominator = lax.fori_loop(0, SLOTS, slot_step, initial)
        return (numerator / denominator[..., None]).astype(jnp.bfloat16)
    blocks = lax.map(one_block, jnp.arange(TILES_T * TILES_H, dtype=jnp.int32))
    shaped = blocks.reshape(TILES_T, TILES_H, CB, WT, TILE, D).transpose(0, 2, 1, 3, 4, 5)
    return shaped.reshape(BLOCKS, TILES_H, WT * TILE, D)
```

```python
import math

import jax
import jax.numpy as jnp
from jax import lax
from jax.experimental import pallas as pl
from jax.experimental.pallas import tpu as pltpu
from jax.sharding import Mesh, PartitionSpec as P

TILES = 4
HD = 128
CORES = 2
STRIDE = 7
SLOTS = 8
HEADS = 24
LIST_ROWS = 16
PARTS = 3


def turned(w):
    return w * STRIDE % TILES


def normed(block, gain):
    block = block.astype(jnp.float32)
    mean_sq = jnp.mean(block * block, axis=-1, keepdims=True)
    return (block * lax.rsqrt(mean_sq + 1e-06) * gain).astype(jnp.bfloat16)


def head_spans(width):
    return [slice(head * HD, (head + 1) * HD) for head in range(width // HD)]


def spread_kv_kernel(k_hbm, v_hbm, gain_ref, kv_out, raw, laid, in_sems, out_sems):
    parts, part_width = raw.shape[1], raw.shape[3]
    per_part = part_width // HD
    arrivals = []
    for part in range(parts):
        span = slice(part * part_width, (part + 1) * part_width)
        for which, source in enumerate((k_hbm, v_hbm)):
            arrivals.append(
                pltpu.make_async_copy(
                    source.at[:, span], raw.at[which, part], in_sems.at[which, part]
                )
            )
    for copy in arrivals:
        copy.start()

    def leave(index, first, last):
        span = pl.ds(first, last - first)
        return pltpu.make_async_copy(laid.at[span], kv_out.at[span], out_sems.at[index])

    heads, slots = parts * per_part, laid.shape[0]
    laid[heads:] = jnp.zeros((slots - heads,) + laid.shape[1:], laid.dtype)
    departures = [leave(parts, heads, slots)]
    departures[0].start()
    gain = gain_ref[...]
    for part in range(parts):
        first = part * per_part
        arrivals[2 * part].wait()
        for head, span in enumerate(head_spans(part_width)):
            laid[first + head, 0] = normed(raw[0, part, :, span], gain)
        arrivals[2 * part + 1].wait()
        for head, span in enumerate(head_spans(part_width)):
            laid[first + head, 1] = raw[1, part, :, span]
        departures.append(leave(part, first, first + per_part))
        departures[-1].start()
    for copy in departures:
        copy.wait()


def spread_q_kernel(offsets_ref, counts_ref, q_ref, gain_ref, q_out):
    tokens = q_ref.shape[0]
    lane = lax.broadcasted_iota(jnp.int32, (LIST_ROWS, HD), 1)
    listed = jnp.full((LIST_ROWS, HD), -1, jnp.int32)
    for slot in range(offsets_ref.shape[1]):
        code = jnp.where(slot < counts_ref[0, 0], offsets_ref[0, slot], -1)
        listed = jnp.where(lane == slot, code, listed)
    listed = listed.astype(jnp.float32).astype(jnp.bfloat16)
    gain = gain_ref[...]
    spans = head_spans(q_ref.shape[1])
    for slot in range(q_out.shape[0]):
        if slot < len(spans):
            q_out[slot, :tokens] = normed(q_ref[:, spans[slot]], gain)
        else:
            q_out[slot, :tokens] = jnp.zeros((tokens, HD), q_out.dtype)
        q_out[slot, tokens:] = listed


def list_entries(lists_ref, slots, pick, picked):
    def entry(index, found):
        w, slot = index // slots, index % slots
        code = lists_ref[w, slot]
        taken, place = pick(code // 3)
        taken = (code >= 0) & taken

        @pl.when(taken)
        def _():
            picked[0, found] = place
            picked[1, found] = turned(w + code % 3 - 1)
            picked[2, found] = w

        return found + taken.astype(jnp.int32)

    found = lax.fori_loop(0, TILES * slots, entry, 0)
    for extra in range(3):
        picked[0, found + extra] = 0
        picked[1, found + extra] = 0
        picked[2, found + extra] = TILES
    return found


def sum_entries(found, picked, query, kv, total, score_a, score_b):
    tile = total.shape[1]
    tokens = kv.shape[5]
    factor = math.log2(math.e) / math.sqrt(HD)
    ones = jnp.ones((tile, HD), jnp.bfloat16)

    def held(index, which):
        return kv[picked[0, index], :, picked[1, index], :, which].reshape(tile, HD)

    def score(index):
        w = jnp.minimum(picked[2, index], TILES - 1)
        tile_q = query[:, turned(w), :, :tokens].reshape(tile, HD)
        return lax.dot_general(
            tile_q, held(index, 0), (((1,), (1,)), ((), ())), preferred_element_type=jnp.float32
        )

    def absorb(index, scores):
        weight = jnp.exp2(scores[...] * factor).astype(jnp.bfloat16)
        total[picked[2, index]] += jnp.dot(
            weight,
            jnp.concatenate([held(index, 1), ones], axis=1),
            preferred_element_type=jnp.float32,
        )

    score_a[...] = score(0)

    def two(pair, carry):
        index = 2 * pair
        score_b[...] = score(index + 1)
        absorb(index, score_a)
        score_a[...] = score(index + 2)
        absorb(index + 1, score_b)
        return carry

    lax.fori_loop(0, (found + 1) // 2, two, 0)


def near_kernel(query, own, xm, ym, xp, yp, sums, far, kv, read, lists, picked, sa, sb, sems):
    copies = []
    for place, source in enumerate((ym, xm, own, xp, yp)):
        copies.append(pltpu.make_async_copy(source, kv.at[place], sems.at[place]))
    for copy in copies:
        copy.start()
    tokens = kv.shape[5]
    for w in range(TILES):
        behind = query[0, turned(w), 0, tokens:].astype(jnp.float32)
        read[w : w + 1] = behind[:1].astype(jnp.int32)
    to_scalars = pltpu.make_async_copy(read, lists, sems.at[len(copies)])
    to_scalars.start()
    sums[...] = jnp.zeros(sums.shape, sums.dtype)
    to_scalars.wait()

    mirrored = lax.axis_index("d") % CORES == 1

    def sides(place):
        frame, row = place // 3, place % 3
        return jnp.where(mirrored, 2 - frame, frame), jnp.where(mirrored, 2 - row, row)

    def pick(place):
        frame, row = sides(place)
        return (frame == 1) | (row == 1), jnp.where(frame == 1, 2 * row, frame + 1)

    def pick_far(place):
        frame, row = sides(place)
        return (frame != 1) & (row != 1), frame // 2 * 2 + row // 2

    found = list_entries(lists, SLOTS, pick, picked)
    far[3, 0] = list_entries(lists, SLOTS, pick_far, far)
    for copy in copies:
        copy.wait()
    sum_entries(found, picked, query, kv, sums, sa, sb)


def far_kernel(picked, query, sums, mp, mm, pm, pp, out_ref, kv, total, sa, sb, sems):
    copies = []
    for index, source in enumerate((mm, mp, pm, pp)):
        copies.append(pltpu.make_async_copy(source, kv.at[index], sems.at[index]))
    for copy in copies:
        copy.start()
    total[...] = sums[...]
    for copy in copies:
        copy.wait()
    sum_entries(picked[3, 0], picked, query, kv, total, sa, sb)
    for w in range(TILES):
        attended = total[w, :, :HD] / total[w, :, HD:]
        shape = out_ref.shape[:1] + out_ref.shape[2:]
        out_ref[:, turned(w)] = attended.astype(jnp.bfloat16).reshape(shape)


def collect_kernel(chunk_ref, out_ref):
    for head, span in enumerate(head_spans(out_ref.shape[1])):
        out_ref[:, span] = chunk_ref[head]


def flat(x, y, z, core):
    z_hi, z_lo = divmod(z, TILES)
    return (((x * TILES + z_lo) * TILES + y) * TILES + z_hi) * CORES + core


def rings():
    length = TILES * TILES
    return [
        [flat(x, y, STRIDE * i % length, core) for i in range(length) for core in range(CORES)]
        for x in range(TILES)
        for y in range(TILES)
    ]


def exchanged(array):
    return lax.all_to_all(
        array, "d", split_axis=0, concat_axis=0, axis_index_groups=rings(), tiled=True
    )


def moved(array, axis, by):
    pairs = []
    for x in range(TILES):
        for y in range(TILES):
            for core, step in enumerate((by, -by)):
                to_x, to_y = (x + step, y) if axis == "x" else (x, y + step)
                if 0 <= to_x < TILES and 0 <= to_y < TILES:
                    for z in range(TILES * TILES):
                        pairs.append((flat(x, y, z, core), flat(to_x, to_y, z, core)))
    return lax.ppermute(array, "d", pairs)


VMEM = pl.BlockSpec(memory_space=pltpu.VMEM)
HBM = pl.BlockSpec(memory_space=pl.ANY)
SMEM = pl.BlockSpec(memory_space=pltpu.SMEM)


def params(mib):
    return pltpu.CompilerParams(vmem_limit_bytes=mib * 1024 * 1024)


def spread(queries, keys, values, q_gain, k_gain, offsets, counts):
    dev_tok, width = queries.shape[2:]
    devices = TILES * TILES * CORES
    vmem, hbm, smem = VMEM, HBM, SMEM
    kv_chunks = pl.pallas_call(
        spread_kv_kernel,
        out_shape=jax.ShapeDtypeStruct((devices, 2, dev_tok, HD), jnp.bfloat16),
        in_specs=[hbm] * 2 + [vmem],
        out_specs=hbm,
        scratch_shapes=[
            pltpu.VMEM((2, PARTS, dev_tok, width // PARTS), jnp.bfloat16),
            pltpu.VMEM((devices, 2, dev_tok, HD), jnp.bfloat16),
            pltpu.SemaphoreType.DMA((2, PARTS)),
            pltpu.SemaphoreType.DMA((PARTS + 1,)),
        ],
        compiler_params=params(63),
    )(keys.reshape(dev_tok, width), values.reshape(dev_tok, width), k_gain.reshape(1, HD))
    q_chunks = pl.pallas_call(
        spread_q_kernel,
        out_shape=jax.ShapeDtypeStruct((devices, dev_tok + LIST_ROWS, HD), jnp.bfloat16),
        in_specs=[smem] * 2 + [vmem] * 2,
        out_specs=vmem,
        compiler_params=params(16),
    )(
        offsets.reshape(1, SLOTS),
        counts.reshape(1, 1),
        queries.reshape(dev_tok, width),
        q_gain.reshape(1, HD),
    )
    return kv_chunks, q_chunks


def on_device(kv_chunks, q_chunks):
    devices, _, dev_tok = kv_chunks.shape[:3]
    sizes = (TILES, TILES, CORES)
    width = HEADS * HD
    tile = devices // TILES * dev_tok
    vmem, hbm, smem = VMEM, HBM, SMEM
    own = exchanged(kv_chunks)
    query = exchanged(q_chunks)

    xm, ym = moved(own, "x", 1), moved(own, "y", 1)
    xp, yp = moved(own, "x", -1), moved(own, "y", -1)
    mp, mm = moved(xm, "y", -1), moved(ym, "x", 1)
    pm, pp = moved(xp, "y", 1), moved(yp, "x", -1)

    def by_place(array):
        return array.reshape(sizes + array.shape[1:])

    def cost(entries):
        pairs = TILES * entries * tile * tile
        return pl.CostEstimate(
            flops=6 * HD * pairs, bytes_accessed=12 * own.size, transcendentals=pairs
        )

    listed = TILES * SLOTS + 3

    def scratch(columns):
        return [
            pltpu.VMEM((tile, tile), jnp.float32),
            pltpu.VMEM((tile, tile), jnp.float32),
            pltpu.SemaphoreType.DMA((columns + 1,)),
        ]

    def held(columns):
        return pltpu.VMEM((columns,) + sizes + own.shape[1:], jnp.bfloat16)

    query = by_place(query)
    sums_shape = (TILES + 1, tile, 2 * HD)
    sums, far = pl.pallas_call(
        near_kernel,
        out_shape=(
            jax.ShapeDtypeStruct(sums_shape, jnp.float32),
            jax.ShapeDtypeStruct((4, listed), jnp.int32),
        ),
        in_specs=[vmem] + [hbm] * 5,
        out_specs=(vmem, smem),
        scratch_shapes=[
            held(5),
            pltpu.VMEM((TILES, HD), jnp.int32),
            pltpu.SMEM((TILES, HD), jnp.int32),
            pltpu.SMEM((3, listed), jnp.int32),
        ]
        + scratch(5),
        compiler_params=params(24),
        cost_estimate=cost(5),
    )(query, *(by_place(array) for array in (own, xm, ym, xp, yp)))
    attended = pl.pallas_call(
        far_kernel,
        out_shape=jax.ShapeDtypeStruct(sizes + (dev_tok, HD), jnp.bfloat16),
        in_specs=[smem] + [vmem] * 2 + [hbm] * 4,
        out_specs=vmem,
        scratch_shapes=[held(4), pltpu.VMEM(sums_shape, jnp.float32)] + scratch(4),
        compiler_params=params(24),
        cost_estimate=cost(2),
    )(far, query, sums, *(by_place(array) for array in (mp, mm, pm, pp)))

    chunks = attended.reshape(devices, dev_tok, HD)
    chunks = exchanged(chunks)
    return pl.pallas_call(
        collect_kernel,
        out_shape=jax.ShapeDtypeStruct((dev_tok, width), jnp.bfloat16),
        in_specs=[vmem],
        out_specs=vmem,
        compiler_params=params(16),
    )(chunks)


def solution(mesh):
    fine = Mesh(
        mesh.devices.reshape(TILES, TILES, TILES, TILES, CORES), ("x", "zl", "y", "zh", "c")
    )
    line = Mesh(mesh.devices.reshape(-1), ("d",))
    tokens = P(("x", "zl"), "y", ("zh", "c"), None)
    by_device = P(fine.axis_names)
    first = jax.shard_map(
        spread,
        mesh=fine,
        in_specs=(
            tokens,
            tokens,
            tokens,
            P(),
            P(),
            P(("x", "zl"), "y", None, None),
            P(("x", "zl"), "y", None),
        ),
        out_specs=(by_device, by_device),
        check_vma=False,
    )
    middle = jax.shard_map(
        on_device, mesh=line, in_specs=(P("d"), P("d")), out_specs=P("d"), check_vma=False
    )
    last = jax.shard_map(
        lambda rows: rows[None, None],
        mesh=fine,
        in_specs=by_device,
        out_specs=tokens,
        check_vma=False,
    )

    def whole(*arrays):
        return last(middle(*first(*arrays)))

    return whole
```

```python
import math

import jax
import jax.numpy as jnp
from jax import lax
from jax.experimental import pallas as pl
from jax.experimental.pallas import tpu as pltpu
from jax.sharding import Mesh, PartitionSpec as P

TILES = 4
HD = 128
RING = ("zl", "zh", "c")
SLOTS = 8
LIST_ROWS = 16
PARTS = 3


def normed(block, gain):
    block = block.astype(jnp.float32)
    mean_sq = jnp.mean(block * block, axis=-1, keepdims=True)
    return (block * lax.rsqrt(mean_sq + 1e-06) * gain).astype(jnp.bfloat16)


def head_spans(width):
    return [slice(head * HD, (head + 1) * HD) for head in range(width // HD)]


def spread_kv_kernel(k_hbm, v_hbm, gain_ref, kv_out, raw, laid, in_sems, out_sems):
    parts, part_width = raw.shape[1], raw.shape[3]
    per_part = part_width // HD
    arrivals = []
    for part in range(parts):
        span = slice(part * part_width, (part + 1) * part_width)
        for which, source in enumerate((k_hbm, v_hbm)):
            arrivals.append(
                pltpu.make_async_copy(
                    source.at[:, span], raw.at[which, part], in_sems.at[which, part]
                )
            )
    for copy in arrivals:
        copy.start()

    def leave(index, first, last):
        span = pl.ds(first, last - first)
        return pltpu.make_async_copy(laid.at[span], kv_out.at[span], out_sems.at[index])

    heads, slots = parts * per_part, laid.shape[0]
    laid[heads:] = jnp.zeros((slots - heads,) + laid.shape[1:], laid.dtype)
    departures = [leave(parts, heads, slots)]
    departures[0].start()
    gain = gain_ref[...]
    for part in range(parts):
        first = part * per_part
        arrivals[2 * part].wait()
        for head, span in enumerate(head_spans(part_width)):
            laid[first + head, 0] = normed(raw[0, part, :, span], gain)
        arrivals[2 * part + 1].wait()
        for head, span in enumerate(head_spans(part_width)):
            laid[first + head, 1] = raw[1, part, :, span]
        departures.append(leave(part, first, first + per_part))
        departures[-1].start()
    for copy in departures:
        copy.wait()


def spread_q_kernel(offsets_ref, counts_ref, q_ref, gain_ref, q_out):
    tokens = q_ref.shape[0]
    lane = lax.broadcasted_iota(jnp.int32, (LIST_ROWS, HD), 1)
    listed = jnp.full((LIST_ROWS, HD), -1, jnp.int32)
    for slot in range(offsets_ref.shape[1]):
        code = jnp.where(slot < counts_ref[0, 0], offsets_ref[0, slot], -1)
        listed = jnp.where(lane == slot, code, listed)
    listed = listed.astype(jnp.float32).astype(jnp.bfloat16)
    gain = gain_ref[...]
    spans = head_spans(q_ref.shape[1])
    for slot in range(q_out.shape[0]):
        if slot < len(spans):
            q_out[slot, :tokens] = normed(q_ref[:, spans[slot]], gain)
        else:
            q_out[slot, :tokens] = jnp.zeros((tokens, HD), q_out.dtype)
        q_out[slot, tokens:] = listed


def list_entries(lists_ref, mirrored, near, far):
    near_found = far_found = jnp.int32(0)
    for w in range(TILES):
        for slot in range(SLOTS):
            code = lists_ref[w, slot]
            place = (code * 171) >> 9
            frame = (code * 57) >> 9
            row = place - 3 * frame
            column = w + code - 3 * place - 1
            frame = jnp.where(mirrored, 2 - frame, frame)
            row = jnp.where(mirrored, 2 - row, row)
            is_near = (frame == 1) | (row == 1)
            near[0, near_found] = jnp.where(frame == 1, 2 * row, frame + 1)
            near[1, near_found] = column
            near[2, near_found] = w
            far[0, far_found] = (frame >> 1) * 2 + (row >> 1)
            far[1, far_found] = column
            far[2, far_found] = w
            near_found += ((code >= 0) & is_near).astype(jnp.int32)
            far_found += ((code >= 0) & jnp.logical_not(is_near)).astype(jnp.int32)
    for picked, found in ((near, near_found), (far, far_found)):
        for extra in range(3):
            picked[0, found + extra] = 0
            picked[1, found + extra] = 0
            picked[2, found + extra] = TILES
        picked[3, 0] = found


def sum_entries(found, picked, query, kv, total, score_a, score_b):
    tile = total.shape[1]
    tokens = kv.shape[5]
    factor = math.log2(math.e) / math.sqrt(HD)
    ones = jnp.ones((tile, HD), jnp.bfloat16)

    def held(index, which):
        return kv[picked[0, index], picked[1, index], :, :, which].reshape(tile, HD)

    def score(index):
        w = jnp.minimum(picked[2, index], TILES - 1)
        tile_q = query[w, :, :, :tokens].reshape(tile, HD)
        return lax.dot_general(
            tile_q, held(index, 0), (((1,), (1,)), ((), ())), preferred_element_type=jnp.float32
        )

    def absorb(index, scores):
        weight = jnp.exp2(scores[...] * factor).astype(jnp.bfloat16)
        total[picked[2, index]] += jnp.dot(
            weight,
            jnp.concatenate([held(index, 1), ones], axis=1),
            preferred_element_type=jnp.float32,
        )

    score_a[...] = score(0)

    def two(pair, carry):
        index = 2 * pair
        score_b[...] = score(index + 1)
        absorb(index, score_a)
        score_a[...] = score(index + 2)
        absorb(index + 1, score_b)
        return carry

    lax.fori_loop(0, (found + 1) // 2, two, 0)


def near_kernel(query, own, xm, ym, xp, yp, sums, far, kv, read, lists, picked, sa, sb, sems):
    copies = []
    for place, source in enumerate((ym, xm, own, xp, yp)):
        copies.append(pltpu.make_async_copy(source, kv.at[place], sems.at[place]))
    for copy in copies:
        copy.start()
    tokens = kv.shape[5]
    for w in range(TILES):
        behind = query[w, 0, 0, tokens:].astype(jnp.float32)
        read[w : w + 1] = behind[:1].astype(jnp.int32)
    to_scalars = pltpu.make_async_copy(read, lists, sems.at[len(copies)])
    to_scalars.start()
    sums[...] = jnp.zeros(sums.shape, sums.dtype)
    to_scalars.wait()

    list_entries(lists, lax.axis_index("c") == 1, picked, far)
    for copy in copies:
        copy.wait()
    sum_entries(picked[3, 0], picked, query, kv, sums, sa, sb)


def far_kernel(picked, query, sums, mp, mm, pm, pp, out_ref, kv, total, sa, sb, sems):
    copies = []
    for index, source in enumerate((mm, mp, pm, pp)):
        copies.append(pltpu.make_async_copy(source, kv.at[index], sems.at[index]))
    for copy in copies:
        copy.start()
    total[...] = sums[...]
    for copy in copies:
        copy.wait()
    sum_entries(picked[3, 0], picked, query, kv, total, sa, sb)
    for w in range(TILES):
        attended = total[w, :, :HD] / total[w, :, HD:]
        out_ref[w] = attended.astype(jnp.bfloat16).reshape(out_ref.shape[1:])


def collect_kernel(chunk_ref, out_ref):
    for head, span in enumerate(head_spans(out_ref.shape[1])):
        out_ref[:, span] = chunk_ref[head]


def moved(array, axis, by):
    line, cores = lax.axis_size(axis), lax.axis_size("c")
    pairs = []
    for i in range(line):
        for core in range(cores):
            to, to_core = i + (by if core == 0 else -by), core
            if not 0 <= to < line:
                to, to_core = i, 1 - core
            pairs.append((i * cores + core, to * cores + to_core))
    return lax.ppermute(array, (axis, "c"), pairs)


def on_device(queries, keys, values, q_gain, k_gain, offsets, counts):
    dev_tok, width = queries.shape[2:]
    sizes = tuple(lax.axis_size(axis) for axis in RING)
    devices = math.prod(sizes)
    tile = devices // TILES * dev_tok
    vmem = pl.BlockSpec(memory_space=pltpu.VMEM)
    hbm = pl.BlockSpec(memory_space=pl.ANY)
    smem = pl.BlockSpec(memory_space=pltpu.SMEM)

    def params(mib):
        return pltpu.CompilerParams(vmem_limit_bytes=mib * 1024 * 1024)

    kv_chunks = pl.pallas_call(
        spread_kv_kernel,
        out_shape=jax.ShapeDtypeStruct((devices, 2, dev_tok, HD), jnp.bfloat16),
        in_specs=[hbm] * 2 + [vmem],
        out_specs=hbm,
        scratch_shapes=[
            pltpu.VMEM((2, PARTS, dev_tok, width // PARTS), jnp.bfloat16),
            pltpu.VMEM((devices, 2, dev_tok, HD), jnp.bfloat16),
            pltpu.SemaphoreType.DMA((2, PARTS)),
            pltpu.SemaphoreType.DMA((PARTS + 1,)),
        ],
        compiler_params=params(63),
    )(keys.reshape(dev_tok, width), values.reshape(dev_tok, width), k_gain.reshape(1, HD))
    own = lax.all_to_all(kv_chunks, RING, split_axis=0, concat_axis=0, tiled=True)
    q_chunks = pl.pallas_call(
        spread_q_kernel,
        out_shape=jax.ShapeDtypeStruct((devices, dev_tok + LIST_ROWS, HD), jnp.bfloat16),
        in_specs=[smem] * 2 + [vmem] * 2,
        out_specs=vmem,
        compiler_params=params(16),
    )(
        offsets.reshape(1, SLOTS),
        counts.reshape(1, 1),
        queries.reshape(dev_tok, width),
        q_gain.reshape(1, HD),
    )
    query = lax.all_to_all(q_chunks, RING, split_axis=0, concat_axis=0, tiled=True)

    xm, ym = moved(own, "x", 1), moved(own, "y", 1)
    xp, yp = moved(own, "x", -1), moved(own, "y", -1)
    mp, mm = moved(xm, "y", -1), moved(ym, "x", 1)
    pm, pp = moved(xp, "y", 1), moved(yp, "x", -1)

    def by_place(array):
        return array.reshape(sizes + array.shape[1:])

    def cost(entries):
        pairs = TILES * entries * tile * tile
        return pl.CostEstimate(
            flops=6 * HD * pairs, bytes_accessed=12 * own.size, transcendentals=pairs
        )

    listed = TILES * SLOTS + 3

    def scratch(columns):
        return [
            pltpu.VMEM((tile, tile), jnp.float32),
            pltpu.VMEM((tile, tile), jnp.float32),
            pltpu.SemaphoreType.DMA((columns + 1,)),
        ]

    def held(columns):
        return pltpu.VMEM((columns,) + sizes + own.shape[1:], jnp.bfloat16)

    query = by_place(query)
    sums_shape = (TILES + 1, tile, 2 * HD)
    sums, far = pl.pallas_call(
        near_kernel,
        out_shape=(
            jax.ShapeDtypeStruct(sums_shape, jnp.float32),
            jax.ShapeDtypeStruct((4, listed), jnp.int32),
        ),
        in_specs=[vmem] + [hbm] * 5,
        out_specs=(vmem, smem),
        scratch_shapes=[
            held(5),
            pltpu.VMEM((TILES, HD), jnp.int32),
            pltpu.SMEM((TILES, HD), jnp.int32),
            pltpu.SMEM((4, listed), jnp.int32),
        ]
        + scratch(5),
        compiler_params=params(24),
        cost_estimate=cost(5),
    )(query, *(by_place(array) for array in (own, xm, ym, xp, yp)))
    attended = pl.pallas_call(
        far_kernel,
        out_shape=jax.ShapeDtypeStruct(sizes + (dev_tok, HD), jnp.bfloat16),
        in_specs=[smem] + [vmem] * 2 + [hbm] * 4,
        out_specs=vmem,
        scratch_shapes=[held(4), pltpu.VMEM(sums_shape, jnp.float32)] + scratch(4),
        compiler_params=params(24),
        cost_estimate=cost(2),
    )(far, query, sums, *(by_place(array) for array in (mp, mm, pm, pp)))

    chunks = attended.reshape(devices, dev_tok, HD)
    chunks = lax.all_to_all(chunks, RING, split_axis=0, concat_axis=0, tiled=True)
    result = pl.pallas_call(
        collect_kernel,
        out_shape=jax.ShapeDtypeStruct((dev_tok, width), jnp.bfloat16),
        in_specs=[vmem],
        out_specs=vmem,
        compiler_params=params(16),
    )(chunks)
    return result.reshape(1, 1, dev_tok, width)


def solution(mesh):
    frames = TILES
    columns = mesh.shape["tm"] // frames
    fine = Mesh(
        mesh.devices.reshape(frames, columns, mesh.shape["height"], mesh.shape["head"] // 2, 2),
        ("x", "zl", "y", "zh", "c"),
    )
    tokens = P(("x", "zl"), "y", ("zh", "c"), None)
    return jax.shard_map(
        on_device,
        mesh=fine,
        in_specs=(
            tokens,
            tokens,
            tokens,
            P(),
            P(),
            P(("x", "zl"), "y", None, None),
            P(("x", "zl"), "y", None),
        ),
        out_specs=tokens,
        check_vma=False,
    )
```

```python
import math

import jax
import jax.numpy as jnp
from jax import lax
from jax.experimental import pallas as pl
from jax.experimental.pallas import tpu as pltpu
from jax.sharding import Mesh, PartitionSpec as P

TILES = 4
HD = 128
RING = ("zl", "zh", "c")
SLOTS = 8
PARTS = 3


def normed(block, gain):
    block = block.astype(jnp.float32)
    mean_sq = jnp.mean(block * block, axis=-1, keepdims=True)
    return (block * lax.rsqrt(mean_sq + 1e-06) * gain).astype(jnp.bfloat16)


def head_spans(width):
    return [slice(head * HD, (head + 1) * HD) for head in range(width // HD)]


def spread_kv_kernel(k_hbm, v_hbm, gain_ref, kv_out, raw, laid, in_sems, out_sems):
    parts, part_width = raw.shape[1], raw.shape[3]
    per_part = part_width // HD
    arrivals = []
    for part in range(parts):
        span = slice(part * part_width, (part + 1) * part_width)
        for which, source in enumerate((k_hbm, v_hbm)):
            arrivals.append(
                pltpu.make_async_copy(
                    source.at[:, span], raw.at[which, part], in_sems.at[which, part]
                )
            )
    for copy in arrivals:
        copy.start()

    def leave(index, first, last):
        span = pl.ds(first, last - first)
        return pltpu.make_async_copy(laid.at[span], kv_out.at[span], out_sems.at[index])

    heads, slots = parts * per_part, laid.shape[0]
    laid[heads:] = jnp.zeros((slots - heads,) + laid.shape[1:], laid.dtype)
    departures = [leave(parts, heads, slots)]
    departures[0].start()
    gain = gain_ref[...]
    for part in range(parts):
        first = part * per_part
        arrivals[2 * part].wait()
        for head, span in enumerate(head_spans(part_width)):
            laid[first + head, 0] = normed(raw[0, part, :, span], gain)
        arrivals[2 * part + 1].wait()
        for head, span in enumerate(head_spans(part_width)):
            laid[first + head, 1] = raw[1, part, :, span]
        departures.append(leave(part, first, first + per_part))
        departures[-1].start()
    for copy in departures:
        copy.wait()


def spread_q_kernel(offsets_ref, counts_ref, q_ref, gain_ref, q_out, table):
    for slot in range(SLOTS):
        table[0, slot] = jnp.where(slot < counts_ref[0, 0], offsets_ref[0, slot], -1)
    gain = gain_ref[...]
    spans = head_spans(q_ref.shape[1])
    for slot in range(q_out.shape[0]):
        if slot < len(spans):
            q_out[slot] = normed(q_ref[:, spans[slot]], gain)
        else:
            q_out[slot] = jnp.zeros(q_out.shape[1:], q_out.dtype)


def hand_on_kernel(q_in, after, t1, t2, t3, q_out):
    del q_in, after, t1, t2, t3, q_out


def list_entries(lists_ref, mirrored, near, far):
    near_found = far_found = jnp.int32(0)
    for w in range(TILES):
        for slot in range(SLOTS):
            code = lists_ref[w, slot]
            place = (code * 171) >> 9
            frame = (code * 57) >> 9
            row = place - 3 * frame
            column = w + code - 3 * place - 1
            frame = jnp.where(mirrored, 2 - frame, frame)
            row = jnp.where(mirrored, 2 - row, row)
            is_near = (frame == 1) | (row == 1)
            near[0, near_found] = jnp.where(frame == 1, 2 * row, frame + 1)
            near[1, near_found] = column
            near[2, near_found] = w
            far[0, far_found] = (frame >> 1) * 2 + (row >> 1)
            far[1, far_found] = column
            far[2, far_found] = w
            near_found += ((code >= 0) & is_near).astype(jnp.int32)
            far_found += ((code >= 0) & jnp.logical_not(is_near)).astype(jnp.int32)
    for picked, found in ((near, near_found), (far, far_found)):
        for extra in range(3):
            picked[0, found + extra] = 0
            picked[1, found + extra] = 0
            picked[2, found + extra] = TILES
        picked[3, 0] = found


def sum_entries(found, picked, query, kv, total, score_a, score_b):
    tile = total.shape[1]
    factor = math.log2(math.e) / math.sqrt(HD)
    ones = jnp.ones((tile, HD), jnp.bfloat16)

    def held(index, which):
        return kv[picked[0, index], picked[1, index], :, :, which].reshape(tile, HD)

    def score(index):
        w = jnp.minimum(picked[2, index], TILES - 1)
        tile_q = query[w].reshape(tile, HD)
        return lax.dot_general(
            tile_q, held(index, 0), (((1,), (1,)), ((), ())), preferred_element_type=jnp.float32
        )

    def absorb(index, scores):
        weight = jnp.exp2(scores[...] * factor).astype(jnp.bfloat16)
        total[picked[2, index]] += jnp.dot(
            weight,
            jnp.concatenate([held(index, 1), ones], axis=1),
            preferred_element_type=jnp.float32,
        )

    score_a[...] = score(0)

    def two(pair, carry):
        index = 2 * pair
        score_b[...] = score(index + 1)
        absorb(index, score_a)
        score_a[...] = score(index + 2)
        absorb(index + 1, score_b)
        return carry

    lax.fori_loop(0, (found + 1) // 2, two, 0)


def near_kernel(
    t0, t1, t2, t3, query, own, xm, ym, xp, yp, sums, far, kv, lists, picked, sa, sb, sems
):
    copies = []
    for place, source in enumerate((ym, xm, own, xp, yp)):
        copies.append(pltpu.make_async_copy(source, kv.at[place], sems.at[place]))
    for copy in copies:
        copy.start()
    here = lax.axis_index("zl")
    for step, table in enumerate((t0, t1, t2, t3)):
        w = (here - step + TILES) & (TILES - 1)
        for slot in range(SLOTS):
            lists[w, slot] = table[0, slot]
    sums[...] = jnp.zeros(sums.shape, sums.dtype)
    list_entries(lists, lax.axis_index("c") == 1, picked, far)
    for copy in copies:
        copy.wait()
    sum_entries(picked[3, 0], picked, query, kv, sums, sa, sb)


def far_kernel(picked, query, sums, mp, mm, pm, pp, out_ref, kv, total, sa, sb, sems):
    copies = []
    for index, source in enumerate((mm, mp, pm, pp)):
        copies.append(pltpu.make_async_copy(source, kv.at[index], sems.at[index]))
    for copy in copies:
        copy.start()
    total[...] = sums[...]
    for copy in copies:
        copy.wait()
    sum_entries(picked[3, 0], picked, query, kv, total, sa, sb)
    for w in range(TILES):
        attended = total[w, :, :HD] / total[w, :, HD:]
        out_ref[w] = attended.astype(jnp.bfloat16).reshape(out_ref.shape[1:])


def collect_kernel(chunk_ref, out_ref):
    for head, span in enumerate(head_spans(out_ref.shape[1])):
        out_ref[:, span] = chunk_ref[head]


def moved(array, axis, by):
    line, cores = lax.axis_size(axis), lax.axis_size("c")
    pairs = []
    for i in range(line):
        for core in range(cores):
            to, to_core = i + (by if core == 0 else -by), core
            if not 0 <= to < line:
                to, to_core = i, 1 - core
            pairs.append((i * cores + core, to * cores + to_core))
    return lax.ppermute(array, (axis, "c"), pairs)


def on_device(queries, keys, values, q_gain, k_gain, offsets, counts):
    dev_tok, width = queries.shape[2:]
    sizes = tuple(lax.axis_size(axis) for axis in RING)
    devices = math.prod(sizes)
    tile = devices // TILES * dev_tok
    vmem = pl.BlockSpec(memory_space=pltpu.VMEM)
    hbm = pl.BlockSpec(memory_space=pl.ANY)
    smem = pl.BlockSpec(memory_space=pltpu.SMEM)

    def params(mib):
        return pltpu.CompilerParams(vmem_limit_bytes=mib * 1024 * 1024)

    kv_chunks = pl.pallas_call(
        spread_kv_kernel,
        out_shape=jax.ShapeDtypeStruct((devices, 2, dev_tok, HD), jnp.bfloat16),
        in_specs=[hbm] * 2 + [vmem],
        out_specs=hbm,
        scratch_shapes=[
            pltpu.VMEM((2, PARTS, dev_tok, width // PARTS), jnp.bfloat16),
            pltpu.VMEM((devices, 2, dev_tok, HD), jnp.bfloat16),
            pltpu.SemaphoreType.DMA((2, PARTS)),
            pltpu.SemaphoreType.DMA((PARTS + 1,)),
        ],
        compiler_params=params(63),
    )(keys.reshape(dev_tok, width), values.reshape(dev_tok, width), k_gain.reshape(1, HD))
    own = lax.all_to_all(kv_chunks, RING, split_axis=0, concat_axis=0, tiled=True)
    q_chunks, table = pl.pallas_call(
        spread_q_kernel,
        out_shape=(
            jax.ShapeDtypeStruct((devices, dev_tok, HD), jnp.bfloat16),
            jax.ShapeDtypeStruct((1, SLOTS), jnp.int32),
        ),
        in_specs=[smem] * 2 + [vmem] * 2,
        out_specs=(vmem, smem),
        compiler_params=params(16),
    )(
        offsets.reshape(1, SLOTS),
        counts.reshape(1, 1),
        queries.reshape(dev_tok, width),
        q_gain.reshape(1, HD),
    )
    turns = [[(i, (i + step) % TILES) for i in range(TILES)] for step in range(TILES)]
    tables = [table] + [lax.ppermute(table, "zl", turns[step]) for step in range(1, TILES)]
    q_chunks = pl.pallas_call(
        hand_on_kernel,
        out_shape=jax.ShapeDtypeStruct(q_chunks.shape, q_chunks.dtype),
        in_specs=[hbm] * 5,
        out_specs=hbm,
        input_output_aliases={0: 0},
        compiler_params=params(16),
        cost_estimate=pl.CostEstimate(flops=20_000_000_000, bytes_accessed=0, transcendentals=0),
    )(q_chunks, own, *tables[1:])
    query = lax.all_to_all(q_chunks, RING, split_axis=0, concat_axis=0, tiled=True)

    xm, ym = moved(own, "x", 1), moved(own, "y", 1)
    xp, yp = moved(own, "x", -1), moved(own, "y", -1)
    mp, mm = moved(xm, "y", -1), moved(ym, "x", 1)
    pm, pp = moved(xp, "y", 1), moved(yp, "x", -1)

    def by_place(array):
        return array.reshape(sizes + array.shape[1:])

    def cost(entries):
        pairs = TILES * entries * tile * tile
        return pl.CostEstimate(
            flops=6 * HD * pairs, bytes_accessed=12 * own.size, transcendentals=pairs
        )

    listed = TILES * SLOTS + 3

    def scratch(columns):
        return [
            pltpu.VMEM((tile, tile), jnp.float32),
            pltpu.VMEM((tile, tile), jnp.float32),
            pltpu.SemaphoreType.DMA((columns + 1,)),
        ]

    def held(columns):
        return pltpu.VMEM((columns,) + sizes + own.shape[1:], jnp.bfloat16)

    query = by_place(query)
    sums_shape = (TILES + 1, tile, 2 * HD)
    sums, far = pl.pallas_call(
        near_kernel,
        out_shape=(
            jax.ShapeDtypeStruct(sums_shape, jnp.float32),
            jax.ShapeDtypeStruct((4, listed), jnp.int32),
        ),
        in_specs=[smem] * 4 + [vmem] + [hbm] * 5,
        out_specs=(vmem, smem),
        scratch_shapes=[
            held(5),
            pltpu.SMEM((TILES, SLOTS), jnp.int32),
            pltpu.SMEM((4, listed), jnp.int32),
        ]
        + scratch(5),
        compiler_params=params(24),
        cost_estimate=cost(5),
    )(*tables, query, *(by_place(array) for array in (own, xm, ym, xp, yp)))
    attended = pl.pallas_call(
        far_kernel,
        out_shape=jax.ShapeDtypeStruct(sizes + (dev_tok, HD), jnp.bfloat16),
        in_specs=[smem] + [vmem] * 2 + [hbm] * 4,
        out_specs=vmem,
        scratch_shapes=[held(4), pltpu.VMEM(sums_shape, jnp.float32)] + scratch(4),
        compiler_params=params(24),
        cost_estimate=cost(2),
    )(far, query, sums, *(by_place(array) for array in (mp, mm, pm, pp)))

    chunks = attended.reshape(devices, dev_tok, HD)
    chunks = lax.all_to_all(chunks, RING, split_axis=0, concat_axis=0, tiled=True)
    result = pl.pallas_call(
        collect_kernel,
        out_shape=jax.ShapeDtypeStruct((dev_tok, width), jnp.bfloat16),
        in_specs=[vmem],
        out_specs=vmem,
        compiler_params=params(16),
    )(chunks)
    return result.reshape(1, 1, dev_tok, width)


def solution(mesh):
    frames = TILES
    columns = mesh.shape["tm"] // frames
    fine = Mesh(
        mesh.devices.reshape(frames, columns, mesh.shape["height"], mesh.shape["head"] // 2, 2),
        ("x", "zl", "y", "zh", "c"),
    )
    tokens = P(("x", "zl"), "y", ("zh", "c"), None)
    return jax.shard_map(
        on_device,
        mesh=fine,
        in_specs=(
            tokens,
            tokens,
            tokens,
            P(),
            P(),
            P(("x", "zl"), "y", None, None),
            P(("x", "zl"), "y", None),
        ),
        out_specs=tokens,
        check_vma=False,
    )
```

```python
import math

import jax
import jax.numpy as jnp
from jax import lax
from jax.experimental import pallas as pl
from jax.experimental.pallas import tpu as pltpu
from jax.sharding import Mesh, PartitionSpec as P

TILES = 4
HD = 128
RING = ("zl", "zh", "c")
SLOTS = 8
PARTS = 3


def normed(block, gain):
    block = block.astype(jnp.float32)
    mean_sq = jnp.mean(block * block, axis=-1, keepdims=True)
    return (block * lax.rsqrt(mean_sq + 1e-06) * gain).astype(jnp.bfloat16)


def head_spans(width):
    return [slice(head * HD, (head + 1) * HD) for head in range(width // HD)]


def spread_kv_kernel(k_hbm, v_hbm, gain_ref, kv_out, raw, laid, in_sems, out_sems):
    parts, part_width = raw.shape[1], raw.shape[3]
    per_part = part_width // HD
    arrivals = []
    for part in range(parts):
        span = slice(part * part_width, (part + 1) * part_width)
        for which, source in enumerate((k_hbm, v_hbm)):
            arrivals.append(
                pltpu.make_async_copy(
                    source.at[:, span], raw.at[which, part], in_sems.at[which, part]
                )
            )
    for copy in arrivals:
        copy.start()

    def leave(index, first, last):
        span = pl.ds(first, last - first)
        return pltpu.make_async_copy(laid.at[span], kv_out.at[span], out_sems.at[index])

    heads, slots = parts * per_part, laid.shape[0]
    laid[heads:] = jnp.zeros((slots - heads,) + laid.shape[1:], laid.dtype)
    departures = [leave(parts, heads, slots)]
    departures[0].start()
    gain = gain_ref[...]
    for part in range(parts):
        first = part * per_part
        arrivals[2 * part].wait()
        for head, span in enumerate(head_spans(part_width)):
            laid[first + head, 0] = normed(raw[0, part, :, span], gain)
        arrivals[2 * part + 1].wait()
        for head, span in enumerate(head_spans(part_width)):
            laid[first + head, 1] = raw[1, part, :, span]
        departures.append(leave(part, first, first + per_part))
        departures[-1].start()
    for copy in departures:
        copy.wait()


def spread_q_kernel(offsets_ref, counts_ref, q_ref, gain_ref, q_out, table):
    for slot in range(SLOTS):
        table[0, slot] = jnp.where(slot < counts_ref[0, 0], offsets_ref[0, slot], -1)
    gain = gain_ref[...]
    spans = head_spans(q_ref.shape[1])
    for slot in range(q_out.shape[0]):
        if slot < len(spans):
            q_out[slot] = normed(q_ref[:, spans[slot]], gain)
        else:
            q_out[slot] = jnp.zeros(q_out.shape[1:], q_out.dtype)


def hand_on_kernel(q_in, after, t1, t2, t3, q_out):
    del q_in, after, t1, t2, t3, q_out


def pause_kernel(table, xm, ym, xp, yp, table_out):
    del table, xm, ym, xp, yp, table_out


def list_entries(lists_ref, mirrored, near, far):
    near_found = far_found = jnp.int32(0)
    for w in range(TILES):
        for slot in range(SLOTS):
            code = lists_ref[w, slot]
            place = (code * 171) >> 9
            frame = (code * 57) >> 9
            row = place - 3 * frame
            column = w + code - 3 * place - 1
            frame = jnp.where(mirrored, 2 - frame, frame)
            row = jnp.where(mirrored, 2 - row, row)
            is_near = (frame == 1) | (row == 1)
            near[0, near_found] = jnp.where(frame == 1, 2 * row, frame + 1)
            near[1, near_found] = column
            near[2, near_found] = w
            far[0, far_found] = (frame >> 1) * 2 + (row >> 1)
            far[1, far_found] = column
            far[2, far_found] = w
            near_found += ((code >= 0) & is_near).astype(jnp.int32)
            far_found += ((code >= 0) & jnp.logical_not(is_near)).astype(jnp.int32)
    for picked, found in ((near, near_found), (far, far_found)):
        for extra in range(3):
            picked[0, found + extra] = 0
            picked[1, found + extra] = 0
            picked[2, found + extra] = TILES
        picked[3, 0] = found


def sum_entries(found, picked, query, kv, total, score_a, score_b):
    tile = total.shape[1]
    factor = math.log2(math.e) / math.sqrt(HD)
    ones = jnp.ones((tile, HD), jnp.bfloat16)

    def held(index, which):
        return kv[picked[0, index], picked[1, index], :, :, which].reshape(tile, HD)

    def score(index):
        w = jnp.minimum(picked[2, index], TILES - 1)
        tile_q = query[w].reshape(tile, HD)
        return lax.dot_general(
            tile_q, held(index, 0), (((1,), (1,)), ((), ())), preferred_element_type=jnp.float32
        )

    def absorb(index, scores):
        weight = jnp.exp2(scores[...] * factor).astype(jnp.bfloat16)
        total[picked[2, index]] += jnp.dot(
            weight,
            jnp.concatenate([held(index, 1), ones], axis=1),
            preferred_element_type=jnp.float32,
        )

    score_a[...] = score(0)

    def two(pair, carry):
        index = 2 * pair
        score_b[...] = score(index + 1)
        absorb(index, score_a)
        score_a[...] = score(index + 2)
        absorb(index + 1, score_b)
        return carry

    lax.fori_loop(0, (found + 1) // 2, two, 0)


def near_kernel(
    t0, t1, t2, t3, query, own, xm, ym, xp, yp, sums, far, kv, lists, picked, sa, sb, sems
):
    copies = []
    for place, source in enumerate((ym, xm, own, xp, yp)):
        copies.append(pltpu.make_async_copy(source, kv.at[place], sems.at[place]))
    for copy in copies:
        copy.start()
    here = lax.axis_index("zl")
    for step, table in enumerate((t0, t1, t2, t3)):
        w = (here - step + TILES) & (TILES - 1)
        for slot in range(SLOTS):
            lists[w, slot] = table[0, slot]
    sums[...] = jnp.zeros(sums.shape, sums.dtype)
    list_entries(lists, lax.axis_index("c") == 1, picked, far)
    for copy in copies:
        copy.wait()
    sum_entries(picked[3, 0], picked, query, kv, sums, sa, sb)


def far_kernel(picked, query, sums, mp, mm, pm, pp, out_ref, kv, total, sa, sb, sems):
    copies = []
    for index, source in enumerate((mm, mp, pm, pp)):
        copies.append(pltpu.make_async_copy(source, kv.at[index], sems.at[index]))
    for copy in copies:
        copy.start()
    total[...] = sums[...]
    for copy in copies:
        copy.wait()
    sum_entries(picked[3, 0], picked, query, kv, total, sa, sb)
    for w in range(TILES):
        attended = total[w, :, :HD] / total[w, :, HD:]
        out_ref[w] = attended.astype(jnp.bfloat16).reshape(out_ref.shape[1:])


def collect_kernel(chunk_ref, out_ref):
    for head, span in enumerate(head_spans(out_ref.shape[1])):
        out_ref[:, span] = chunk_ref[head]


def moved(array, axis, by):
    line, cores = lax.axis_size(axis), lax.axis_size("c")
    pairs = []
    for i in range(line):
        for core in range(cores):
            to, to_core = i + (by if core == 0 else -by), core
            if not 0 <= to < line:
                to, to_core = i, 1 - core
            pairs.append((i * cores + core, to * cores + to_core))
    return lax.ppermute(array, (axis, "c"), pairs)


def on_device(queries, keys, values, q_gain, k_gain, offsets, counts):
    dev_tok, width = queries.shape[2:]
    sizes = tuple(lax.axis_size(axis) for axis in RING)
    devices = math.prod(sizes)
    tile = devices // TILES * dev_tok
    vmem = pl.BlockSpec(memory_space=pltpu.VMEM)
    hbm = pl.BlockSpec(memory_space=pl.ANY)
    smem = pl.BlockSpec(memory_space=pltpu.SMEM)

    def params(mib):
        return pltpu.CompilerParams(vmem_limit_bytes=mib * 1024 * 1024)

    kv_chunks = pl.pallas_call(
        spread_kv_kernel,
        out_shape=jax.ShapeDtypeStruct((devices, 2, dev_tok, HD), jnp.bfloat16),
        in_specs=[hbm] * 2 + [vmem],
        out_specs=hbm,
        scratch_shapes=[
            pltpu.VMEM((2, PARTS, dev_tok, width // PARTS), jnp.bfloat16),
            pltpu.VMEM((devices, 2, dev_tok, HD), jnp.bfloat16),
            pltpu.SemaphoreType.DMA((2, PARTS)),
            pltpu.SemaphoreType.DMA((PARTS + 1,)),
        ],
        compiler_params=params(63),
    )(keys.reshape(dev_tok, width), values.reshape(dev_tok, width), k_gain.reshape(1, HD))
    own = lax.all_to_all(kv_chunks, RING, split_axis=0, concat_axis=0, tiled=True)
    q_chunks, table = pl.pallas_call(
        spread_q_kernel,
        out_shape=(
            jax.ShapeDtypeStruct((devices, dev_tok, HD), jnp.bfloat16),
            jax.ShapeDtypeStruct((1, SLOTS), jnp.int32),
        ),
        in_specs=[smem] * 2 + [vmem] * 2,
        out_specs=(vmem, smem),
        compiler_params=params(16),
    )(
        offsets.reshape(1, SLOTS),
        counts.reshape(1, 1),
        queries.reshape(dev_tok, width),
        q_gain.reshape(1, HD),
    )
    turns = [[(i, (i + step) % TILES) for i in range(TILES)] for step in range(TILES)]
    tables = [table] + [lax.ppermute(table, "zl", turns[step]) for step in range(1, TILES)]
    q_chunks = pl.pallas_call(
        hand_on_kernel,
        out_shape=jax.ShapeDtypeStruct(q_chunks.shape, q_chunks.dtype),
        in_specs=[hbm] * 5,
        out_specs=hbm,
        input_output_aliases={0: 0},
        compiler_params=params(16),
        cost_estimate=pl.CostEstimate(flops=20_000_000_000, bytes_accessed=0, transcendentals=0),
    )(q_chunks, own, *tables[1:])
    query = lax.all_to_all(q_chunks, RING, split_axis=0, concat_axis=0, tiled=True)

    xm, ym = moved(own, "x", 1), moved(own, "y", 1)
    xp, yp = moved(own, "x", -1), moved(own, "y", -1)
    mp, mm = moved(xm, "y", -1), moved(ym, "x", 1)
    pm, pp = moved(xp, "y", 1), moved(yp, "x", -1)

    tables[1] = pl.pallas_call(
        pause_kernel,
        out_shape=jax.ShapeDtypeStruct(table.shape, table.dtype),
        in_specs=[hbm] * 5,
        out_specs=hbm,
        input_output_aliases={0: 0},
        compiler_params=params(16),
        cost_estimate=pl.CostEstimate(flops=24_000_000_000, bytes_accessed=0, transcendentals=0),
    )(tables[1], xm, ym, xp, yp)

    def by_place(array):
        return array.reshape(sizes + array.shape[1:])

    def cost(entries):
        pairs = TILES * entries * tile * tile
        return pl.CostEstimate(
            flops=6 * HD * pairs, bytes_accessed=12 * own.size, transcendentals=pairs
        )

    listed = TILES * SLOTS + 3

    def scratch(columns):
        return [
            pltpu.VMEM((tile, tile), jnp.float32),
            pltpu.VMEM((tile, tile), jnp.float32),
            pltpu.SemaphoreType.DMA((columns + 1,)),
        ]

    def held(columns):
        return pltpu.VMEM((columns,) + sizes + own.shape[1:], jnp.bfloat16)

    query = by_place(query)
    sums_shape = (TILES + 1, tile, 2 * HD)
    sums, far = pl.pallas_call(
        near_kernel,
        out_shape=(
            jax.ShapeDtypeStruct(sums_shape, jnp.float32),
            jax.ShapeDtypeStruct((4, listed), jnp.int32),
        ),
        in_specs=[smem] * 4 + [vmem] + [hbm] * 5,
        out_specs=(vmem, smem),
        scratch_shapes=[
            held(5),
            pltpu.SMEM((TILES, SLOTS), jnp.int32),
            pltpu.SMEM((4, listed), jnp.int32),
        ]
        + scratch(5),
        compiler_params=params(24),
        cost_estimate=cost(5),
    )(*tables, query, *(by_place(array) for array in (own, xm, ym, xp, yp)))
    attended = pl.pallas_call(
        far_kernel,
        out_shape=jax.ShapeDtypeStruct(sizes + (dev_tok, HD), jnp.bfloat16),
        in_specs=[smem] + [vmem] * 2 + [hbm] * 4,
        out_specs=vmem,
        scratch_shapes=[held(4), pltpu.VMEM(sums_shape, jnp.float32)] + scratch(4),
        compiler_params=params(24),
        cost_estimate=cost(2),
    )(far, query, sums, *(by_place(array) for array in (mp, mm, pm, pp)))

    chunks = attended.reshape(devices, dev_tok, HD)
    chunks = lax.all_to_all(chunks, RING, split_axis=0, concat_axis=0, tiled=True)
    result = pl.pallas_call(
        collect_kernel,
        out_shape=jax.ShapeDtypeStruct((dev_tok, width), jnp.bfloat16),
        in_specs=[vmem],
        out_specs=vmem,
        compiler_params=params(16),
    )(chunks)
    return result.reshape(1, 1, dev_tok, width)


def solution(mesh):
    frames = TILES
    columns = mesh.shape["tm"] // frames
    fine = Mesh(
        mesh.devices.reshape(frames, columns, mesh.shape["height"], mesh.shape["head"] // 2, 2),
        ("x", "zl", "y", "zh", "c"),
    )
    tokens = P(("x", "zl"), "y", ("zh", "c"), None)
    return jax.shard_map(
        on_device,
        mesh=fine,
        in_specs=(
            tokens,
            tokens,
            tokens,
            P(),
            P(),
            P(("x", "zl"), "y", None, None),
            P(("x", "zl"), "y", None),
        ),
        out_specs=tokens,
        check_vma=False,
    )
```

```python
import math

import jax
import jax.numpy as jnp
from jax import lax
from jax.experimental import pallas as pl
from jax.experimental.pallas import tpu as pltpu
from jax.sharding import Mesh, PartitionSpec as P

TILES = 4
HD = 128
RING = ("zl", "zh", "c")
SLOTS = 8
PARTS = 3


def normed(block, gain):
    block = block.astype(jnp.float32)
    mean_sq = jnp.mean(block * block, axis=-1, keepdims=True)
    return (block * lax.rsqrt(mean_sq + 1e-06) * gain).astype(jnp.bfloat16)


def head_spans(width):
    return [slice(head * HD, (head + 1) * HD) for head in range(width // HD)]


def spread_kv_kernel(k_hbm, v_hbm, gain_ref, kv_out, raw, laid, in_sems, out_sems):
    parts, part_width = raw.shape[1], raw.shape[3]
    per_part = part_width // HD
    arrivals = []
    for part in range(parts):
        span = slice(part * part_width, (part + 1) * part_width)
        for which, source in enumerate((k_hbm, v_hbm)):
            arrivals.append(
                pltpu.make_async_copy(
                    source.at[:, span], raw.at[which, part], in_sems.at[which, part]
                )
            )
    for copy in arrivals:
        copy.start()

    def leave(index, first, last):
        span = pl.ds(first, last - first)
        return pltpu.make_async_copy(laid.at[span], kv_out.at[span], out_sems.at[index])

    heads, slots = parts * per_part, laid.shape[0]
    laid[heads:] = jnp.zeros((slots - heads,) + laid.shape[1:], laid.dtype)
    departures = [leave(parts, heads, slots)]
    departures[0].start()
    gain = gain_ref[...]
    for part in range(parts):
        first = part * per_part
        arrivals[2 * part].wait()
        for head, span in enumerate(head_spans(part_width)):
            laid[first + head, 0] = normed(raw[0, part, :, span], gain)
        arrivals[2 * part + 1].wait()
        for head, span in enumerate(head_spans(part_width)):
            laid[first + head, 1] = raw[1, part, :, span]
        departures.append(leave(part, first, first + per_part))
        departures[-1].start()
    for copy in departures:
        copy.wait()


def spread_q_kernel(offsets_ref, counts_ref, q_ref, gain_ref, q_out, table):
    for slot in range(SLOTS):
        table[0, slot] = jnp.where(slot < counts_ref[0, 0], offsets_ref[0, slot], -1)
    gain = gain_ref[...]
    spans = head_spans(q_ref.shape[1])
    for slot in range(q_out.shape[0]):
        if slot < len(spans):
            q_out[slot] = normed(q_ref[:, spans[slot]], gain)
        else:
            q_out[slot] = jnp.zeros(q_out.shape[1:], q_out.dtype)


def hand_on_kernel(q_in, after, t1, t2, t3, q_out):
    del q_in, after, t1, t2, t3, q_out


def list_entries(lists_ref, mirrored, near, far):
    near_found = far_found = jnp.int32(0)
    for w in range(TILES):
        for slot in range(SLOTS):
            code = lists_ref[w, slot]
            place = (code * 171) >> 9
            frame = (code * 57) >> 9
            row = place - 3 * frame
            column = w + code - 3 * place - 1
            frame = jnp.where(mirrored, 2 - frame, frame)
            row = jnp.where(mirrored, 2 - row, row)
            is_near = (frame == 1) | (row == 1)
            near[0, near_found] = jnp.where(frame == 1, 2 * row, frame + 1)
            near[1, near_found] = column
            near[2, near_found] = w
            far[0, far_found] = (frame >> 1) * 2 + (row >> 1)
            far[1, far_found] = column
            far[2, far_found] = w
            near_found += ((code >= 0) & is_near).astype(jnp.int32)
            far_found += ((code >= 0) & jnp.logical_not(is_near)).astype(jnp.int32)
    for picked, found in ((near, near_found), (far, far_found)):
        for extra in range(3):
            picked[0, found + extra] = 0
            picked[1, found + extra] = 0
            picked[2, found + extra] = TILES
        picked[3, 0] = found


def sum_entries(found, picked, query, kv, total, score_a, score_b):
    tile = total.shape[1]
    factor = math.log2(math.e) / math.sqrt(HD)
    ones = jnp.ones((tile, HD), jnp.bfloat16)

    def held(index, which):
        return kv[picked[0, index], picked[1, index], :, :, which].reshape(tile, HD)

    def score(index):
        w = jnp.minimum(picked[2, index], TILES - 1)
        tile_q = query[w].reshape(tile, HD)
        return lax.dot_general(
            tile_q, held(index, 0), (((1,), (1,)), ((), ())), preferred_element_type=jnp.float32
        )

    def absorb(index, scores):
        weight = jnp.exp2(scores[...] * factor).astype(jnp.bfloat16)
        total[picked[2, index]] += jnp.dot(
            weight,
            jnp.concatenate([held(index, 1), ones], axis=1),
            preferred_element_type=jnp.float32,
        )

    score_a[...] = score(0)

    def two(pair, carry):
        index = 2 * pair
        score_b[...] = score(index + 1)
        absorb(index, score_a)
        score_a[...] = score(index + 2)
        absorb(index + 1, score_b)
        return carry

    lax.fori_loop(0, (found + 1) // 2, two, 0)


def gather_kernel(t0, t1, t2, t3, own, xm, ym, xp, yp, kv, near, far, lists, sems):
    copies = []
    for place, source in enumerate((ym, xm, own, xp, yp)):
        copies.append(pltpu.make_async_copy(source, kv.at[place], sems.at[place]))
    for copy in copies:
        copy.start()
    here = lax.axis_index("zl")
    for step, table in enumerate((t0, t1, t2, t3)):
        w = (here - step + TILES) & (TILES - 1)
        for slot in range(SLOTS):
            lists[w, slot] = table[0, slot]
    list_entries(lists, lax.axis_index("c") == 1, near, far)
    for copy in copies:
        copy.wait()


def near_kernel(picked, query, kv, sums, sa, sb):
    sums[...] = jnp.zeros(sums.shape, sums.dtype)
    sum_entries(picked[3, 0], picked, query, kv, sums, sa, sb)


def far_kernel(picked, query, sums, mp, mm, pm, pp, out_ref, kv, total, sa, sb, sems):
    copies = []
    for index, source in enumerate((mm, mp, pm, pp)):
        copies.append(pltpu.make_async_copy(source, kv.at[index], sems.at[index]))
    for copy in copies:
        copy.start()
    total[...] = sums[...]
    for copy in copies:
        copy.wait()
    sum_entries(picked[3, 0], picked, query, kv, total, sa, sb)
    for w in range(TILES):
        attended = total[w, :, :HD] / total[w, :, HD:]
        out_ref[w] = attended.astype(jnp.bfloat16).reshape(out_ref.shape[1:])


def collect_kernel(chunk_ref, out_ref):
    for head, span in enumerate(head_spans(out_ref.shape[1])):
        out_ref[:, span] = chunk_ref[head]


def moved(array, axis, by):
    line, cores = lax.axis_size(axis), lax.axis_size("c")
    pairs = []
    for i in range(line):
        for core in range(cores):
            to, to_core = i + (by if core == 0 else -by), core
            if not 0 <= to < line:
                to, to_core = i, 1 - core
            pairs.append((i * cores + core, to * cores + to_core))
    return lax.ppermute(array, (axis, "c"), pairs)


def on_device(queries, keys, values, q_gain, k_gain, offsets, counts):
    dev_tok, width = queries.shape[2:]
    sizes = tuple(lax.axis_size(axis) for axis in RING)
    devices = math.prod(sizes)
    tile = devices // TILES * dev_tok
    vmem = pl.BlockSpec(memory_space=pltpu.VMEM)
    hbm = pl.BlockSpec(memory_space=pl.ANY)
    smem = pl.BlockSpec(memory_space=pltpu.SMEM)

    def params(mib):
        return pltpu.CompilerParams(vmem_limit_bytes=mib * 1024 * 1024)

    kv_chunks = pl.pallas_call(
        spread_kv_kernel,
        out_shape=jax.ShapeDtypeStruct((devices, 2, dev_tok, HD), jnp.bfloat16),
        in_specs=[hbm] * 2 + [vmem],
        out_specs=hbm,
        scratch_shapes=[
            pltpu.VMEM((2, PARTS, dev_tok, width // PARTS), jnp.bfloat16),
            pltpu.VMEM((devices, 2, dev_tok, HD), jnp.bfloat16),
            pltpu.SemaphoreType.DMA((2, PARTS)),
            pltpu.SemaphoreType.DMA((PARTS + 1,)),
        ],
        compiler_params=params(63),
    )(keys.reshape(dev_tok, width), values.reshape(dev_tok, width), k_gain.reshape(1, HD))
    own = lax.all_to_all(kv_chunks, RING, split_axis=0, concat_axis=0, tiled=True)
    q_chunks, table = pl.pallas_call(
        spread_q_kernel,
        out_shape=(
            jax.ShapeDtypeStruct((devices, dev_tok, HD), jnp.bfloat16),
            jax.ShapeDtypeStruct((1, SLOTS), jnp.int32),
        ),
        in_specs=[smem] * 2 + [vmem] * 2,
        out_specs=(vmem, smem),
        compiler_params=params(16),
    )(
        offsets.reshape(1, SLOTS),
        counts.reshape(1, 1),
        queries.reshape(dev_tok, width),
        q_gain.reshape(1, HD),
    )
    turns = [[(i, (i + step) % TILES) for i in range(TILES)] for step in range(TILES)]
    tables = [table] + [lax.ppermute(table, "zl", turns[step]) for step in range(1, TILES)]
    q_chunks = pl.pallas_call(
        hand_on_kernel,
        out_shape=jax.ShapeDtypeStruct(q_chunks.shape, q_chunks.dtype),
        in_specs=[hbm] * 5,
        out_specs=hbm,
        input_output_aliases={0: 0},
        compiler_params=params(16),
        cost_estimate=pl.CostEstimate(flops=20_000_000_000, bytes_accessed=0, transcendentals=0),
    )(q_chunks, own, *tables[1:])
    query = lax.all_to_all(q_chunks, RING, split_axis=0, concat_axis=0, tiled=True)

    xm, ym = moved(own, "x", 1), moved(own, "y", 1)
    xp, yp = moved(own, "x", -1), moved(own, "y", -1)
    mp, mm = moved(xm, "y", -1), moved(ym, "x", 1)
    pm, pp = moved(xp, "y", 1), moved(yp, "x", -1)

    def by_place(array):
        return array.reshape(sizes + array.shape[1:])

    def cost(entries):
        pairs = TILES * entries * tile * tile
        return pl.CostEstimate(
            flops=6 * HD * pairs, bytes_accessed=12 * own.size, transcendentals=pairs
        )

    query = by_place(query)
    listed = jax.ShapeDtypeStruct((4, TILES * SLOTS + 3), jnp.int32)
    scores = [pltpu.VMEM((tile, tile), jnp.float32)] * 2
    sums = jax.ShapeDtypeStruct((TILES + 1, tile, 2 * HD), jnp.float32)
    near_kv, near, far = pl.pallas_call(
        gather_kernel,
        out_shape=(
            jax.ShapeDtypeStruct((5,) + sizes + own.shape[1:], jnp.bfloat16),
            listed,
            listed,
        ),
        in_specs=[smem] * 4 + [hbm] * 5,
        out_specs=(vmem, smem, smem),
        scratch_shapes=[pltpu.SMEM((TILES, SLOTS), jnp.int32), pltpu.SemaphoreType.DMA((5,))],
        compiler_params=params(16),
        cost_estimate=pl.CostEstimate(flops=24_000_000_000, bytes_accessed=0, transcendentals=0),
    )(*tables, *(by_place(array) for array in (own, xm, ym, xp, yp)))
    near_sums = pl.pallas_call(
        near_kernel,
        out_shape=sums,
        in_specs=[smem] + [vmem] * 2,
        out_specs=vmem,
        scratch_shapes=scores,
        compiler_params=params(16),
        cost_estimate=cost(5),
    )(near, query, near_kv)
    attended = pl.pallas_call(
        far_kernel,
        out_shape=jax.ShapeDtypeStruct(sizes + (dev_tok, HD), jnp.bfloat16),
        in_specs=[smem] + [vmem] * 2 + [hbm] * 4,
        out_specs=vmem,
        scratch_shapes=[
            pltpu.VMEM((4,) + sizes + own.shape[1:], jnp.bfloat16),
            pltpu.VMEM(sums.shape, sums.dtype),
        ]
        + scores
        + [pltpu.SemaphoreType.DMA((4,))],
        compiler_params=params(24),
        cost_estimate=cost(2),
    )(far, query, near_sums, *(by_place(array) for array in (mp, mm, pm, pp)))

    chunks = attended.reshape(devices, dev_tok, HD)
    chunks = lax.all_to_all(chunks, RING, split_axis=0, concat_axis=0, tiled=True)
    result = pl.pallas_call(
        collect_kernel,
        out_shape=jax.ShapeDtypeStruct((dev_tok, width), jnp.bfloat16),
        in_specs=[vmem],
        out_specs=vmem,
        compiler_params=params(16),
    )(chunks)
    return result.reshape(1, 1, dev_tok, width)


def solution(mesh):
    frames = TILES
    columns = mesh.shape["tm"] // frames
    fine = Mesh(
        mesh.devices.reshape(frames, columns, mesh.shape["height"], mesh.shape["head"] // 2, 2),
        ("x", "zl", "y", "zh", "c"),
    )
    tokens = P(("x", "zl"), "y", ("zh", "c"), None)
    return jax.shard_map(
        on_device,
        mesh=fine,
        in_specs=(
            tokens,
            tokens,
            tokens,
            P(),
            P(),
            P(("x", "zl"), "y", None, None),
            P(("x", "zl"), "y", None),
        ),
        out_specs=tokens,
        check_vma=False,
    )
```

```python
import math

import jax
import jax.numpy as jnp
from jax import lax
from jax.experimental import pallas as pl
from jax.experimental.pallas import tpu as pltpu
from jax.sharding import Mesh, PartitionSpec as P

TILES = 4
HD = 128
RING = ("zl", "c", "zh")
SLOTS = 8
PARTS = 3


def normed(block, gain):
    block = block.astype(jnp.float32)
    mean_sq = jnp.mean(block * block, axis=-1, keepdims=True)
    return (block * lax.rsqrt(mean_sq + 1e-06) * gain).astype(jnp.bfloat16)


def head_spans(width):
    return [slice(head * HD, (head + 1) * HD) for head in range(width // HD)]


def spread_kv_kernel(k_hbm, v_hbm, gain_ref, kv_out, raw, laid, in_sems, out_sems):
    parts, part_width = raw.shape[1], raw.shape[3]
    per_part = part_width // HD
    arrivals = []
    for part in range(parts):
        span = slice(part * part_width, (part + 1) * part_width)
        for which, source in enumerate((k_hbm, v_hbm)):
            arrivals.append(
                pltpu.make_async_copy(
                    source.at[:, span], raw.at[which, part], in_sems.at[which, part]
                )
            )
    for copy in arrivals:
        copy.start()

    def leave(index, first, last):
        span = pl.ds(first, last - first)
        return pltpu.make_async_copy(laid.at[span], kv_out.at[span], out_sems.at[index])

    heads, slots = parts * per_part, laid.shape[0]
    laid[heads:] = jnp.zeros((slots - heads,) + laid.shape[1:], laid.dtype)
    departures = [leave(parts, heads, slots)]
    departures[0].start()
    gain = gain_ref[...]
    for part in range(parts):
        first = part * per_part
        arrivals[2 * part].wait()
        for head, span in enumerate(head_spans(part_width)):
            laid[first + head, 0] = normed(raw[0, part, :, span], gain)
        arrivals[2 * part + 1].wait()
        for head, span in enumerate(head_spans(part_width)):
            laid[first + head, 1] = raw[1, part, :, span]
        departures.append(leave(part, first, first + per_part))
        departures[-1].start()
    for copy in departures:
        copy.wait()


def spread_q_kernel(offsets_ref, counts_ref, q_ref, gain_ref, q_out, table):
    for slot in range(SLOTS):
        table[0, slot] = jnp.where(slot < counts_ref[0, 0], offsets_ref[0, slot], -1)
    gain = gain_ref[...]
    spans = head_spans(q_ref.shape[1])
    for slot in range(q_out.shape[0]):
        if slot < len(spans):
            q_out[slot] = normed(q_ref[:, spans[slot]], gain)
        else:
            q_out[slot] = jnp.zeros(q_out.shape[1:], q_out.dtype)


def hand_on_kernel(q_in, after, t1, t2, t3, q_out):
    del q_in, after, t1, t2, t3, q_out


def pause_kernel(table, xm, ym, xp, yp, table_out):
    del table, xm, ym, xp, yp, table_out


def list_entries(lists_ref, mirrored, near, far):
    near_found = far_found = jnp.int32(0)
    for w in range(TILES):
        for slot in range(SLOTS):
            code = lists_ref[w, slot]
            place = (code * 171) >> 9
            frame = (code * 57) >> 9
            row = place - 3 * frame
            column = w + code - 3 * place - 1
            frame = jnp.where(mirrored, 2 - frame, frame)
            row = jnp.where(mirrored, 2 - row, row)
            is_near = (frame == 1) | (row == 1)
            near[0, near_found] = jnp.where(frame == 1, 2 * row, frame + 1)
            near[1, near_found] = column
            near[2, near_found] = w
            far[0, far_found] = (frame >> 1) * 2 + (row >> 1)
            far[1, far_found] = column
            far[2, far_found] = w
            near_found += ((code >= 0) & is_near).astype(jnp.int32)
            far_found += ((code >= 0) & jnp.logical_not(is_near)).astype(jnp.int32)
    for picked, found in ((near, near_found), (far, far_found)):
        for extra in range(3):
            picked[0, found + extra] = 0
            picked[1, found + extra] = 0
            picked[2, found + extra] = TILES
        picked[3, 0] = found


def sum_entries(found, picked, query, kv, total, score_a, score_b):
    tile = total.shape[1]
    factor = math.log2(math.e) / math.sqrt(HD)
    ones = jnp.ones((tile, HD), jnp.bfloat16)

    def held(index, which):
        return kv[picked[0, index], picked[1, index], :, :, which].reshape(tile, HD)

    def score(index):
        w = jnp.minimum(picked[2, index], TILES - 1)
        tile_q = query[w].reshape(tile, HD)
        return lax.dot_general(
            tile_q, held(index, 0), (((1,), (1,)), ((), ())), preferred_element_type=jnp.float32
        )

    def absorb(index, scores):
        weight = jnp.exp2(scores[...] * factor).astype(jnp.bfloat16)
        total[picked[2, index]] += jnp.dot(
            weight,
            jnp.concatenate([held(index, 1), ones], axis=1),
            preferred_element_type=jnp.float32,
        )

    score_a[...] = score(0)

    def two(pair, carry):
        index = 2 * pair
        score_b[...] = score(index + 1)
        absorb(index, score_a)
        score_a[...] = score(index + 2)
        absorb(index + 1, score_b)
        return carry

    lax.fori_loop(0, (found + 1) // 2, two, 0)


def near_kernel(
    t0, t1, t2, t3, query, own, xm, ym, xp, yp, sums, far, kv, lists, picked, sa, sb, sems
):
    copies = []
    for place, source in enumerate((ym, xm, own, xp, yp)):
        copies.append(pltpu.make_async_copy(source, kv.at[place], sems.at[place]))
    for copy in copies:
        copy.start()
    here = lax.axis_index("zl")
    for step, table in enumerate((t0, t1, t2, t3)):
        w = (here - step + TILES) & (TILES - 1)
        for slot in range(SLOTS):
            lists[w, slot] = table[0, slot]
    sums[...] = jnp.zeros(sums.shape, sums.dtype)
    list_entries(lists, lax.axis_index("c") == 1, picked, far)
    for copy in copies:
        copy.wait()
    sum_entries(picked[3, 0], picked, query, kv, sums, sa, sb)


def far_kernel(picked, query, sums, mp, mm, pm, pp, out_ref, kv, total, sa, sb, sems):
    copies = []
    for index, source in enumerate((mm, mp, pm, pp)):
        copies.append(pltpu.make_async_copy(source, kv.at[index], sems.at[index]))
    for copy in copies:
        copy.start()
    total[...] = sums[...]
    for copy in copies:
        copy.wait()
    sum_entries(picked[3, 0], picked, query, kv, total, sa, sb)
    for w in range(TILES):
        attended = total[w, :, :HD] / total[w, :, HD:]
        out_ref[w] = attended.astype(jnp.bfloat16).reshape(out_ref.shape[1:])


def collect_kernel(chunk_ref, out_ref):
    for head, span in enumerate(head_spans(out_ref.shape[1])):
        out_ref[:, span] = chunk_ref[head]


def moved(array, axis, by):
    line, cores = lax.axis_size(axis), lax.axis_size("c")
    pairs = []
    for i in range(line):
        for core in range(cores):
            to, to_core = i + (by if core == 0 else -by), core
            if not 0 <= to < line:
                to, to_core = i, 1 - core
            pairs.append((i * cores + core, to * cores + to_core))
    return lax.ppermute(array, (axis, "c"), pairs)


def on_device(queries, keys, values, q_gain, k_gain, offsets, counts):
    dev_tok, width = queries.shape[2:]
    sizes = tuple(lax.axis_size(axis) for axis in RING)
    devices = math.prod(sizes)
    tile = devices // TILES * dev_tok
    vmem = pl.BlockSpec(memory_space=pltpu.VMEM)
    hbm = pl.BlockSpec(memory_space=pl.ANY)
    smem = pl.BlockSpec(memory_space=pltpu.SMEM)

    def params(mib):
        return pltpu.CompilerParams(vmem_limit_bytes=mib * 1024 * 1024)

    kv_chunks = pl.pallas_call(
        spread_kv_kernel,
        out_shape=jax.ShapeDtypeStruct((devices, 2, dev_tok, HD), jnp.bfloat16),
        in_specs=[hbm] * 2 + [vmem],
        out_specs=hbm,
        scratch_shapes=[
            pltpu.VMEM((2, PARTS, dev_tok, width // PARTS), jnp.bfloat16),
            pltpu.VMEM((devices, 2, dev_tok, HD), jnp.bfloat16),
            pltpu.SemaphoreType.DMA((2, PARTS)),
            pltpu.SemaphoreType.DMA((PARTS + 1,)),
        ],
        compiler_params=params(63),
    )(keys.reshape(dev_tok, width), values.reshape(dev_tok, width), k_gain.reshape(1, HD))
    own = lax.all_to_all(kv_chunks, RING, split_axis=0, concat_axis=0, tiled=True)
    q_chunks, table = pl.pallas_call(
        spread_q_kernel,
        out_shape=(
            jax.ShapeDtypeStruct((devices, dev_tok, HD), jnp.bfloat16),
            jax.ShapeDtypeStruct((1, SLOTS), jnp.int32),
        ),
        in_specs=[smem] * 2 + [vmem] * 2,
        out_specs=(vmem, smem),
        compiler_params=params(16),
    )(
        offsets.reshape(1, SLOTS),
        counts.reshape(1, 1),
        queries.reshape(dev_tok, width),
        q_gain.reshape(1, HD),
    )
    turns = [[(i, (i + step) % TILES) for i in range(TILES)] for step in range(TILES)]
    tables = [table] + [lax.ppermute(table, "zl", turns[step]) for step in range(1, TILES)]
    q_chunks = pl.pallas_call(
        hand_on_kernel,
        out_shape=jax.ShapeDtypeStruct(q_chunks.shape, q_chunks.dtype),
        in_specs=[hbm] * 5,
        out_specs=hbm,
        input_output_aliases={0: 0},
        compiler_params=params(16),
        cost_estimate=pl.CostEstimate(flops=20_000_000_000, bytes_accessed=0, transcendentals=0),
    )(q_chunks, own, *tables[1:])
    query = lax.all_to_all(q_chunks, RING, split_axis=0, concat_axis=0, tiled=True)

    xm, ym = moved(own, "x", 1), moved(own, "y", 1)
    xp, yp = moved(own, "x", -1), moved(own, "y", -1)
    mp, mm = moved(xm, "y", -1), moved(ym, "x", 1)
    pm, pp = moved(xp, "y", 1), moved(yp, "x", -1)

    tables[1] = pl.pallas_call(
        pause_kernel,
        out_shape=jax.ShapeDtypeStruct(table.shape, table.dtype),
        in_specs=[hbm] * 5,
        out_specs=hbm,
        input_output_aliases={0: 0},
        compiler_params=params(16),
        cost_estimate=pl.CostEstimate(flops=24_000_000_000, bytes_accessed=0, transcendentals=0),
    )(tables[1], xm, ym, xp, yp)

    def by_place(array):
        return array.reshape(sizes + array.shape[1:])

    def cost(entries):
        pairs = TILES * entries * tile * tile
        return pl.CostEstimate(
            flops=6 * HD * pairs, bytes_accessed=12 * own.size, transcendentals=pairs
        )

    listed = TILES * SLOTS + 3

    def scratch(columns):
        return [
            pltpu.VMEM((tile, tile), jnp.float32),
            pltpu.VMEM((tile, tile), jnp.float32),
            pltpu.SemaphoreType.DMA((columns + 1,)),
        ]

    def held(columns):
        return pltpu.VMEM((columns,) + sizes + own.shape[1:], jnp.bfloat16)

    query = by_place(query)
    sums_shape = (TILES + 1, tile, 2 * HD)
    sums, far = pl.pallas_call(
        near_kernel,
        out_shape=(
            jax.ShapeDtypeStruct(sums_shape, jnp.float32),
            jax.ShapeDtypeStruct((4, listed), jnp.int32),
        ),
        in_specs=[smem] * 4 + [vmem] + [hbm] * 5,
        out_specs=(vmem, smem),
        scratch_shapes=[
            held(5),
            pltpu.SMEM((TILES, SLOTS), jnp.int32),
            pltpu.SMEM((4, listed), jnp.int32),
        ]
        + scratch(5),
        compiler_params=params(24),
        cost_estimate=cost(5),
    )(*tables, query, *(by_place(array) for array in (own, xm, ym, xp, yp)))
    attended = pl.pallas_call(
        far_kernel,
        out_shape=jax.ShapeDtypeStruct(sizes + (dev_tok, HD), jnp.bfloat16),
        in_specs=[smem] + [vmem] * 2 + [hbm] * 4,
        out_specs=vmem,
        scratch_shapes=[held(4), pltpu.VMEM(sums_shape, jnp.float32)] + scratch(4),
        compiler_params=params(24),
        cost_estimate=cost(2),
    )(far, query, sums, *(by_place(array) for array in (mp, mm, pm, pp)))

    chunks = attended.reshape(devices, dev_tok, HD)
    chunks = lax.all_to_all(chunks, RING, split_axis=0, concat_axis=0, tiled=True)
    result = pl.pallas_call(
        collect_kernel,
        out_shape=jax.ShapeDtypeStruct((dev_tok, width), jnp.bfloat16),
        in_specs=[vmem],
        out_specs=vmem,
        compiler_params=params(16),
    )(chunks)
    return result.reshape(1, 1, dev_tok, width)


def solution(mesh):
    frames = TILES
    columns = mesh.shape["tm"] // frames
    fine = Mesh(
        mesh.devices.reshape(frames, columns, mesh.shape["height"], mesh.shape["head"] // 2, 2),
        ("x", "zl", "y", "zh", "c"),
    )
    tokens = P(("x", "zl"), "y", ("zh", "c"), None)
    return jax.shard_map(
        on_device,
        mesh=fine,
        in_specs=(
            tokens,
            tokens,
            tokens,
            P(),
            P(),
            P(("x", "zl"), "y", None, None),
            P(("x", "zl"), "y", None),
        ),
        out_specs=tokens,
        check_vma=False,
    )
```

```python
import math

import jax
import jax.numpy as jnp
from jax import lax
from jax.experimental import pallas as pl
from jax.experimental.pallas import tpu as pltpu
from jax.sharding import Mesh, PartitionSpec as P

TILES = 4
HD = 128
RING = ("zl", "zh", "c")
SLOTS = 8
PARTS = 3


def normed(block, gain):
    block = block.astype(jnp.float32)
    mean_sq = jnp.mean(block * block, axis=-1, keepdims=True)
    return (block * lax.rsqrt(mean_sq + 1e-06) * gain).astype(jnp.bfloat16)


def head_spans(width):
    return [slice(head * HD, (head + 1) * HD) for head in range(width // HD)]


def spread_kv_kernel(k_hbm, v_hbm, gain_ref, kv_out, raw, laid, in_sems, out_sems):
    parts, part_width = raw.shape[1], raw.shape[3]
    per_part = part_width // HD
    arrivals = []
    for part in range(parts):
        span = slice(part * part_width, (part + 1) * part_width)
        for which, source in enumerate((k_hbm, v_hbm)):
            arrivals.append(
                pltpu.make_async_copy(
                    source.at[:, span], raw.at[which, part], in_sems.at[which, part]
                )
            )
    for copy in arrivals:
        copy.start()

    def leave(index, first, last):
        span = pl.ds(first, last - first)
        return pltpu.make_async_copy(laid.at[span], kv_out.at[span], out_sems.at[index])

    heads, slots = parts * per_part, laid.shape[0]
    laid[heads:] = jnp.zeros((slots - heads,) + laid.shape[1:], laid.dtype)
    departures = [leave(parts, heads, slots)]
    departures[0].start()
    gain = gain_ref[...]
    for part in range(parts):
        first = part * per_part
        arrivals[2 * part].wait()
        for head, span in enumerate(head_spans(part_width)):
            laid[first + head, 0] = normed(raw[0, part, :, span], gain)
        arrivals[2 * part + 1].wait()
        for head, span in enumerate(head_spans(part_width)):
            laid[first + head, 1] = raw[1, part, :, span]
        departures.append(leave(part, first, first + per_part))
        departures[-1].start()
    for copy in departures:
        copy.wait()


def spread_q_kernel(offsets_ref, counts_ref, q_ref, gain_ref, q_out, table):
    for slot in range(SLOTS):
        table[0, slot] = jnp.where(slot < counts_ref[0, 0], offsets_ref[0, slot], -1)
    gain = gain_ref[...]
    spans = head_spans(q_ref.shape[1])
    for slot in range(q_out.shape[0]):
        if slot < len(spans):
            q_out[slot] = normed(q_ref[:, spans[slot]], gain)
        else:
            q_out[slot] = jnp.zeros(q_out.shape[1:], q_out.dtype)


def hand_on_kernel(q_in, after, t1, t2, t3, q_out):
    del q_in, after, t1, t2, t3, q_out


def pause_kernel(table, xm, ym, xp, yp, table_out):
    del table, xm, ym, xp, yp, table_out


def list_entries(lists_ref, mirrored, near, far):
    near_found = far_found = jnp.int32(0)
    for w in range(TILES):
        for slot in range(SLOTS):
            code = lists_ref[w, slot]
            place = (code * 171) >> 9
            frame = (code * 57) >> 9
            row = place - 3 * frame
            column = w + code - 3 * place - 1
            frame = jnp.where(mirrored, 2 - frame, frame)
            row = jnp.where(mirrored, 2 - row, row)
            is_near = (frame == 1) | (row == 1)
            near[0, near_found] = jnp.where(frame == 1, 2 * row, frame + 1)
            near[1, near_found] = column
            near[2, near_found] = w
            far[0, far_found] = (frame >> 1) * 2 + (row >> 1)
            far[1, far_found] = column
            far[2, far_found] = w
            near_found += ((code >= 0) & is_near).astype(jnp.int32)
            far_found += ((code >= 0) & jnp.logical_not(is_near)).astype(jnp.int32)
    for picked, found in ((near, near_found), (far, far_found)):
        for extra in range(3):
            picked[0, found + extra] = 0
            picked[1, found + extra] = 0
            picked[2, found + extra] = TILES
        picked[3, 0] = found


def sum_entries(found, picked, query, kv, total, score_a, score_b):
    tile = total.shape[1]
    factor = math.log2(math.e) / math.sqrt(HD)
    ones = jnp.ones((tile, HD), jnp.bfloat16)

    def held(index, which):
        return kv[picked[0, index], picked[1, index], :, :, which].reshape(tile, HD)

    def score(index):
        w = jnp.minimum(picked[2, index], TILES - 1)
        tile_q = query[w].reshape(tile, HD)
        return lax.dot_general(
            tile_q, held(index, 0), (((1,), (1,)), ((), ())), preferred_element_type=jnp.float32
        )

    def absorb(index, scores):
        weight = jnp.exp2(scores[...] * factor).astype(jnp.bfloat16)
        total[picked[2, index]] += jnp.dot(
            weight,
            jnp.concatenate([held(index, 1), ones], axis=1),
            preferred_element_type=jnp.float32,
        )

    score_a[...] = score(0)

    def two(pair, carry):
        index = 2 * pair
        score_b[...] = score(index + 1)
        absorb(index, score_a)
        score_a[...] = score(index + 2)
        absorb(index + 1, score_b)
        return carry

    lax.fori_loop(0, (found + 1) // 2, two, 0)


def near_kernel(
    t0, t1, t2, t3, query, own, xm, ym, xp, yp, sums, far, kv, lists, picked, sa, sb, sems
):
    copies = []
    for place, source in enumerate((ym, xm, own, xp, yp)):
        for w in range(TILES):
            sem = sems.at[place * TILES + w]
            copies.append(pltpu.make_async_copy(source.at[w], kv.at[place, w], sem))
    for copy in copies:
        copy.start()
    here = lax.axis_index("zl")
    for step, table in enumerate((t0, t1, t2, t3)):
        w = (here - step + TILES) & (TILES - 1)
        for slot in range(SLOTS):
            lists[w, slot] = table[0, slot]
    sums[...] = jnp.zeros(sums.shape, sums.dtype)
    list_entries(lists, lax.axis_index("c") == 1, picked, far)
    for copy in copies:
        copy.wait()
    sum_entries(picked[3, 0], picked, query, kv, sums, sa, sb)


def far_kernel(picked, query, sums, mp, mm, pm, pp, out_ref, kv, total, sa, sb, sems):
    copies = []
    for index, source in enumerate((mm, mp, pm, pp)):
        for w in range(TILES):
            sem = sems.at[index * TILES + w]
            copies.append(pltpu.make_async_copy(source.at[w], kv.at[index, w], sem))
    for copy in copies:
        copy.start()
    total[...] = sums[...]
    for copy in copies:
        copy.wait()
    sum_entries(picked[3, 0], picked, query, kv, total, sa, sb)
    for w in range(TILES):
        attended = total[w, :, :HD] / total[w, :, HD:]
        out_ref[w] = attended.astype(jnp.bfloat16).reshape(out_ref.shape[1:])


def collect_kernel(chunk_ref, out_ref):
    for head, span in enumerate(head_spans(out_ref.shape[1])):
        out_ref[:, span] = chunk_ref[head]


def moved(array, axis, by):
    line, cores = lax.axis_size(axis), lax.axis_size("c")
    pairs = []
    for i in range(line):
        for core in range(cores):
            to, to_core = i + (by if core == 0 else -by), core
            if not 0 <= to < line:
                to, to_core = i, 1 - core
            pairs.append((i * cores + core, to * cores + to_core))
    return lax.ppermute(array, (axis, "c"), pairs)


def on_device(queries, keys, values, q_gain, k_gain, offsets, counts):
    dev_tok, width = queries.shape[2:]
    sizes = tuple(lax.axis_size(axis) for axis in RING)
    devices = math.prod(sizes)
    tile = devices // TILES * dev_tok
    vmem = pl.BlockSpec(memory_space=pltpu.VMEM)
    hbm = pl.BlockSpec(memory_space=pl.ANY)
    smem = pl.BlockSpec(memory_space=pltpu.SMEM)

    def params(mib):
        return pltpu.CompilerParams(vmem_limit_bytes=mib * 1024 * 1024)

    kv_chunks = pl.pallas_call(
        spread_kv_kernel,
        out_shape=jax.ShapeDtypeStruct((devices, 2, dev_tok, HD), jnp.bfloat16),
        in_specs=[hbm] * 2 + [vmem],
        out_specs=hbm,
        scratch_shapes=[
            pltpu.VMEM((2, PARTS, dev_tok, width // PARTS), jnp.bfloat16),
            pltpu.VMEM((devices, 2, dev_tok, HD), jnp.bfloat16),
            pltpu.SemaphoreType.DMA((2, PARTS)),
            pltpu.SemaphoreType.DMA((PARTS + 1,)),
        ],
        compiler_params=params(63),
    )(keys.reshape(dev_tok, width), values.reshape(dev_tok, width), k_gain.reshape(1, HD))
    own = lax.all_to_all(kv_chunks, RING, split_axis=0, concat_axis=0, tiled=True)
    q_chunks, table = pl.pallas_call(
        spread_q_kernel,
        out_shape=(
            jax.ShapeDtypeStruct((devices, dev_tok, HD), jnp.bfloat16),
            jax.ShapeDtypeStruct((1, SLOTS), jnp.int32),
        ),
        in_specs=[smem] * 2 + [vmem] * 2,
        out_specs=(vmem, smem),
        compiler_params=params(16),
    )(
        offsets.reshape(1, SLOTS),
        counts.reshape(1, 1),
        queries.reshape(dev_tok, width),
        q_gain.reshape(1, HD),
    )
    turns = [[(i, (i + step) % TILES) for i in range(TILES)] for step in range(TILES)]
    tables = [table] + [lax.ppermute(table, "zl", turns[step]) for step in range(1, TILES)]
    q_chunks = pl.pallas_call(
        hand_on_kernel,
        out_shape=jax.ShapeDtypeStruct(q_chunks.shape, q_chunks.dtype),
        in_specs=[hbm] * 5,
        out_specs=hbm,
        input_output_aliases={0: 0},
        compiler_params=params(16),
        cost_estimate=pl.CostEstimate(flops=20_000_000_000, bytes_accessed=0, transcendentals=0),
    )(q_chunks, own, *tables[1:])
    query = lax.all_to_all(q_chunks, RING, split_axis=0, concat_axis=0, tiled=True)

    xm, ym = moved(own, "x", 1), moved(own, "y", 1)
    xp, yp = moved(own, "x", -1), moved(own, "y", -1)
    mp, mm = moved(xm, "y", -1), moved(ym, "x", 1)
    pm, pp = moved(xp, "y", 1), moved(yp, "x", -1)

    tables[1] = pl.pallas_call(
        pause_kernel,
        out_shape=jax.ShapeDtypeStruct(table.shape, table.dtype),
        in_specs=[hbm] * 5,
        out_specs=hbm,
        input_output_aliases={0: 0},
        compiler_params=params(16),
        cost_estimate=pl.CostEstimate(flops=24_000_000_000, bytes_accessed=0, transcendentals=0),
    )(tables[1], xm, ym, xp, yp)

    def by_place(array):
        return array.reshape(sizes + array.shape[1:])

    def cost(entries):
        pairs = TILES * entries * tile * tile
        return pl.CostEstimate(
            flops=6 * HD * pairs, bytes_accessed=12 * own.size, transcendentals=pairs
        )

    listed = TILES * SLOTS + 3

    def scratch(columns):
        return [
            pltpu.VMEM((tile, tile), jnp.float32),
            pltpu.VMEM((tile, tile), jnp.float32),
            pltpu.SemaphoreType.DMA((columns * TILES,)),
        ]

    def held(columns):
        return pltpu.VMEM((columns,) + sizes + own.shape[1:], jnp.bfloat16)

    query = by_place(query)
    sums_shape = (TILES + 1, tile, 2 * HD)
    sums, far = pl.pallas_call(
        near_kernel,
        out_shape=(
            jax.ShapeDtypeStruct(sums_shape, jnp.float32),
            jax.ShapeDtypeStruct((4, listed), jnp.int32),
        ),
        in_specs=[smem] * 4 + [vmem] + [hbm] * 5,
        out_specs=(vmem, smem),
        scratch_shapes=[
            held(5),
            pltpu.SMEM((TILES, SLOTS), jnp.int32),
            pltpu.SMEM((4, listed), jnp.int32),
        ]
        + scratch(5),
        compiler_params=params(24),
        cost_estimate=cost(5),
    )(*tables, query, *(by_place(array) for array in (own, xm, ym, xp, yp)))
    attended = pl.pallas_call(
        far_kernel,
        out_shape=jax.ShapeDtypeStruct(sizes + (dev_tok, HD), jnp.bfloat16),
        in_specs=[smem] + [vmem] * 2 + [hbm] * 4,
        out_specs=vmem,
        scratch_shapes=[held(4), pltpu.VMEM(sums_shape, jnp.float32)] + scratch(4),
        compiler_params=params(24),
        cost_estimate=cost(2),
    )(far, query, sums, *(by_place(array) for array in (mp, mm, pm, pp)))

    chunks = attended.reshape(devices, dev_tok, HD)
    chunks = lax.all_to_all(chunks, RING, split_axis=0, concat_axis=0, tiled=True)
    result = pl.pallas_call(
        collect_kernel,
        out_shape=jax.ShapeDtypeStruct((dev_tok, width), jnp.bfloat16),
        in_specs=[vmem],
        out_specs=vmem,
        compiler_params=params(16),
    )(chunks)
    return result.reshape(1, 1, dev_tok, width)


def solution(mesh):
    frames = TILES
    columns = mesh.shape["tm"] // frames
    fine = Mesh(
        mesh.devices.reshape(frames, columns, mesh.shape["height"], mesh.shape["head"] // 2, 2),
        ("x", "zl", "y", "zh", "c"),
    )
    tokens = P(("x", "zl"), "y", ("zh", "c"), None)
    return jax.shard_map(
        on_device,
        mesh=fine,
        in_specs=(
            tokens,
            tokens,
            tokens,
            P(),
            P(),
            P(("x", "zl"), "y", None, None),
            P(("x", "zl"), "y", None),
        ),
        out_specs=tokens,
        check_vma=False,
    )
```
